32 devices in a mesh: row: 4 (over z), col: 8 (over y, x, core).
Axes of the slice: x: 2, y: 2, z: 4, core: 2. Of those that a mesh axis runs over, the one named last changes fastest.
Arguments:
- protocols: float32 [20, 4096], P(None, ('row', 'col')), may hold values from -6 to 6
- w_in: float32 [20, 256], replicated, may hold values from -1.25 to 1.25
- b_in: float32 [256], replicated, may hold values from -3 to 3
- w_out: float32 [256, 64], replicated, may hold values from -0.21875 to 0.21875
- solved: float32 [32, 4096], P(None, ('row', 'col')), may hold values from -0.5 to 0.5
- probes: float32 [32, 4096], P(None, ('row', 'col')), may hold values from -6 to 6
- window_blocks: int32 [4], replicated, may hold values from 0 to 7
Outputs:
- col_grad: float32 [64, 4096], P(None, ('row', 'col'))
- grad_in: float32 [20, 256], replicated
- grad_bias: float32 [256], replicated
- grad_out: float32 [256, 64], replicated
The draws below stay inside these ranges and needn't reach their ends.
Inputs may be any that keep to these rules, and one draw needn't show every extreme that they name: Window block r is the 128 protocols held at index r of row and index window_blocks[r] of col.
All inputs are finite; a program needn't handle non-finite values.
Results may differ from the reference program's by a relative error of at most 0.0003.
Values sent between devices are 32-bit elements; how exact they have to be, the bound alone decides.
No kernel may reach another device: no remote copies, remote signals or barrier semaphores. Data moves between devices by JAX's collectives and lax.ppermute only.
A program may use at most 64 MiB of HBM per device.

```python
import jax
import jax.numpy as jnp
from jax import lax

P_SIZE = 20
H = 256
F = 64
Q = 32
CD = 128
GROUPS = 4
WIN = 512
N = 4096
N_ROW = 4
N_COL = 8


def place_ends(result, key, least, high):
    longest = result.shape.index(max(result.shape))
    spots = []
    for shift in (0, 1):
        where = [jax.random.randint(jax.random.fold_in(key, axis), (), 0, length) for axis, length in enumerate(result.shape)]
        where[longest] = (where[longest] + shift) % result.shape[longest]
        spots.append(tuple(where))
    return result.at[spots[0]].set(least).at[spots[1]].set(high)


def levels(key, shape, shards, low, high):
    def one(position, parts):
        steps = jax.random.uniform(jax.random.fold_in(jax.random.fold_in(key, 6), position), (parts,), jnp.float32, low / len(shards), high / len(shards))
        return jnp.repeat(jnp.exp(steps), shape[position] // parts).reshape((-1,) + (1,) * (len(shape) - position - 1))

    factor_of = one(*shards[0])
    for cut in shards[1:]:
        factor_of = factor_of * one(*cut)
    return factor_of


def centred(key, extent, deviation, bound, shards=(), kind=jnp.bfloat16):
    drawn = jax.random.normal(key, extent, jnp.float32) * deviation
    if len(shards) > 0:
        drawn = levels(key, extent, shards, -0.22, 0.18) * drawn
    return jnp.clip(drawn, min=-bound, max=bound).astype(kind)


def setup_inputs(seed: int = 0) -> dict:
    seeds = jax.random.split(jax.random.key(seed), 8)
    protocols = centred(seeds[0], (P_SIZE, N), 1.0, 6.0, ((1, 32),), jnp.float32)
    w_in = centred(seeds[1], (P_SIZE, H), P_SIZE ** -0.5, 1.25, (), jnp.float32)
    b_in = centred(seeds[2], (H,), 0.5, 3.0, (), jnp.float32)
    w_out = centred(seeds[3], (H, F), (H * 25 // 9) ** -0.5, 0.21875, (), jnp.float32)
    solved = centred(seeds[4], (Q, N), 0.08, 0.5, ((1, 32),), jnp.float32)
    probes = centred(seeds[5], (Q, N), 1.0, 6.0, ((1, 32),), jnp.float32)
    window_blocks = place_ends(jax.random.randint(seeds[6], (GROUPS,), 0, N_COL), jax.random.fold_in(seeds[6], 1), 0, N_COL - 1).astype(jnp.int32)
    return dict(protocols=protocols, w_in=w_in, b_in=b_in, w_out=w_out, solved=solved, probes=probes, window_blocks=window_blocks)


HIGHEST = lax.Precision.HIGHEST


def tile_pass(first_feat, first_vec, second_feat, second_vec):
    first_norm = jnp.sum(first_feat * first_feat, 0)
    second_norm = jnp.sum(second_feat * second_feat, 0)
    cross = jnp.einsum("fi,fj->ij", first_feat, second_feat, precision=HIGHEST)
    kern = jnp.exp(-0.5 * (first_norm[:, None] + second_norm[None, :] - 2.0 * cross))
    weigh = jnp.einsum("qi,qj->ij", first_vec, second_vec, precision=HIGHEST) * kern
    first_grad = jnp.einsum("fj,ij->fi", second_feat, weigh, precision=HIGHEST) - first_feat * jnp.sum(weigh, 1)[None, :]
    second_grad = jnp.einsum("fi,ij->fj", first_feat, weigh, precision=HIGHEST) - second_feat * jnp.sum(weigh, 0)[None, :]
    return first_grad, second_grad


def hidden_of(w_in, b_in, inputs):
    return jnp.tanh(jnp.einsum("ph,pn->hn", w_in, inputs, precision=HIGHEST) + b_in[:, None])


def backprop(w_in, w_out, inputs, hidden, grads):
    grad_out = jnp.einsum("hn,fn->hf", hidden, grads, precision=HIGHEST)
    grad_hidden = jnp.einsum("hf,fn->hn", w_out, grads, precision=HIGHEST)
    grad_pre = grad_hidden * (1.0 - hidden * hidden)
    grad_in = jnp.einsum("pn,hn->ph", inputs, grad_pre, precision=HIGHEST)
    return grad_in, jnp.sum(grad_pre, 1), grad_out


def reference(protocols, w_in, b_in, w_out, solved, probes, window_blocks):
    hidden = hidden_of(w_in, b_in, protocols)
    features = jnp.einsum("hf,hn->fn", w_out, hidden, precision=HIGHEST)
    starts = (jnp.arange(N_ROW, dtype=jnp.int32) * N_COL + window_blocks.astype(jnp.int32)) * CD
    window_cols = (starts[:, None] + jnp.arange(CD, dtype=jnp.int32)[None, :]).reshape(-1).astype(jnp.int32)
    win_feat = features[:, window_cols]
    win_vec = solved[:, window_cols]
    count = N // CD
    feat_blocks = features.reshape(F, count, CD).transpose(1, 0, 2)
    probe_blocks = probes.reshape(Q, count, CD).transpose(1, 0, 2)

    def advance(running, pair):
        win_part, col_part = tile_pass(win_feat, win_vec, pair[0], pair[1])
        return running + win_part, col_part

    win_grad, col_parts = lax.scan(advance, jnp.zeros((F, WIN), jnp.float32), (feat_blocks, probe_blocks))
    col_grad = col_parts.transpose(1, 0, 2).reshape(F, N)
    total = col_grad.at[:, window_cols].add(win_grad)
    grad_in, grad_bias, grad_out = backprop(w_in, w_out, protocols, hidden, total)
    return col_grad, grad_in, grad_bias, grad_out
```

```python
import jax
import jax.numpy as jnp
from jax import lax
from jax.sharding import PartitionSpec as P

HIGHEST = lax.Precision.HIGHEST


def swap(value, axis, size, bit):
    return lax.ppermute(value, axis, [(i, i ^ bit) for i in range(size)])


def bits_of(size):
    return [1 << k for k in range(size.bit_length() - 1)]


def hidden_of(w_in, b_in, inputs):
    return jnp.tanh(jnp.einsum("ph,pn->hn", w_in, inputs, precision=HIGHEST) + b_in[:, None])


def weight_grads(w_in, b_in, w_out, win_in, solved, col_in, probes):
    inputs = jnp.concatenate([win_in, col_in], 1)
    hidden = hidden_of(w_in, b_in, inputs)
    features = jnp.einsum("hf,hn->fn", w_out, hidden, precision=HIGHEST)
    wide = win_in.shape[1]
    first, second = features[:, :wide], features[:, wide:]
    first_norm = jnp.sum(first * first, 0)
    second_norm = jnp.sum(second * second, 0)
    cross = jnp.einsum("fi,fj->ij", first, second, precision=HIGHEST)
    kern = jnp.exp(-0.5 * (first_norm[:, None] + second_norm[None, :] - 2.0 * cross))
    weigh = jnp.einsum("qi,qj->ij", solved, probes, precision=HIGHEST) * kern
    first_grad = jnp.einsum("fj,ij->fi", second, weigh, precision=HIGHEST) - first * jnp.sum(weigh, 1)[None, :]
    second_grad = jnp.einsum("fi,ij->fj", first, weigh, precision=HIGHEST) - second * jnp.sum(weigh, 0)[None, :]
    grads = jnp.concatenate([first_grad, second_grad], 1)
    grad_out = jnp.einsum("hn,fn->fh", hidden, grads, precision=HIGHEST)
    grad_pre = jnp.einsum("hf,fn->hn", w_out, grads, precision=HIGHEST) * (1.0 - hidden * hidden)
    grad_in = jnp.einsum("pn,hn->ph", inputs, grad_pre, precision=HIGHEST)
    return second_grad, grad_in, jnp.sum(grad_pre, 1), grad_out


def body(n_row, n_col, protocols, w_in, b_in, w_out, solved, probes, window_blocks):
    depth, vecs, own = protocols.shape[0], solved.shape[0], protocols.shape[1]
    apart = lax.axis_index("col") ^ window_blocks[lax.axis_index("row")]
    bits = bits_of(n_col)
    shared, joined = bits[:-1], bits[-1]

    def nearer(bit, mine, theirs):
        return jnp.where((apart & bit) == 0, mine, theirs)

    window = jnp.concatenate([protocols, solved])
    columns = jnp.concatenate([protocols, probes])
    for bit in shared:
        window = nearer(bit, window, swap(window, "col", n_col, bit))
    high = window.shape[0]
    got = swap(jnp.concatenate([window, columns]), "col", n_col, joined)
    window = nearer(joined, window, got[:high])
    blocks = jnp.concatenate([window, columns, got[high:]])[None]
    for bit in reversed(bits_of(n_row)):
        blocks = jnp.concatenate([blocks, swap(blocks, "row", n_row, bit)])

    def laid(start, count):
        part = blocks[:, start : start + count]
        return part.transpose(1, 0, 2).reshape(count, -1)

    win_in, win_vec = laid(0, depth), laid(depth, vecs)
    col_in = jnp.concatenate([laid(high, depth), laid(2 * high, depth)], 1)
    col_vec = jnp.concatenate([laid(high + depth, vecs), laid(2 * high + depth, vecs)], 1)
    col_grad, grad_in, grad_bias, grad_out = weight_grads(w_in, b_in, w_out, win_in, win_vec, col_in, col_vec)
    pack = jnp.concatenate([grad_out, grad_in, grad_bias[None]])
    for bit in reversed(shared):
        pack = pack + swap(pack, "col", n_col, bit)
    feats = grad_out.shape[0]
    return (col_grad[:, :own], pack[feats : feats + depth], pack[feats + depth], pack[:feats].T)


def solution(mesh):
    n_row, n_col = mesh.shape["row"], mesh.shape["col"]
    split = P(None, ("row", "col"))

    def per_device(*args):
        return body(n_row, n_col, *args)

    return jax.shard_map(
        per_device,
        mesh=mesh,
        in_specs=(split, P(), P(), P(), split, split, P()),
        out_specs=(split, P(), P(), P()),
        check_vma=False,
    )
```

```python
import functools

import jax
import jax.numpy as jnp
from jax import lax
from jax.experimental import pallas as pl
from jax.experimental.pallas import tpu as pltpu
from jax.sharding import PartitionSpec as P

BF, F32 = jnp.bfloat16, jnp.float32
VMEM = pltpu.VMEM


def swap(value, axis, size, bit):
    return lax.ppermute(value, axis, [(i, i ^ bit) for i in range(size)])


def bits_of(size):
    return [1 << k for k in range(size.bit_length() - 1)]


def split(value, terms=2):
    parts = []
    for _ in range(terms):
        part = value.astype(BF).astype(F32)
        parts.append(part)
        value = value - part
    return parts


def stack(parts):
    return jnp.concatenate(parts, 0).astype(BF)


def mm(a, b):
    return lax.dot_general(a, b, (((1,), (0,)), ((), ())), preferred_element_type=F32)


def mm_nt(a, b):
    return lax.dot_general(a, b, (((1,), (1,)), ((), ())), preferred_element_type=F32)


def mm_tn(a, b):
    return lax.dot_general(a, b, (((0,), (0,)), ((), ())), preferred_element_type=F32)


def each(count, step):
    if count <= 8:
        for i in range(count):
            step(i)
    else:
        lax.fori_loop(0, count, lambda i, c: (step(i), c)[1], 0)


def up(value, to):
    return -(-value // to) * to


class Sizes:
    def __init__(self, depth, vecs, hid, feats, own, n_row):
        self.depth, self.vecs, self.hid, self.feats, self.own, self.n_row = depth, vecs, hid, feats, own, n_row
        self.ins = up(depth + 1, 8)
        self.part = self.ins + vecs
        self.wide = n_row * own
        self.total = 3 * self.wide


def prepare_kernel(z, blocks_ref, protocols_ref, solved_ref, probes_ref, window_ref, columns_ref, apart_ref):
    ones = jnp.where(lax.broadcasted_iota(jnp.int32, (z.ins - z.depth, z.own), 0) == 0, 1.0, 0.0)
    inputs = jnp.concatenate([protocols_ref[...], ones], 0)
    window_ref[: z.ins] = inputs
    window_ref[z.ins :] = solved_ref[...]
    columns_ref[: z.ins] = inputs
    columns_ref[z.ins :] = probes_ref[...]
    apart = blocks_ref[lax.axis_index("row")] ^ lax.axis_index("col")
    apart_ref[...] = jnp.full(apart_ref.shape, apart, jnp.int32)


def compute_kernel(
    z, blocks_ref, w_in_ref, b_in_ref, w_out_ref, col_grad_ref, pack_ref,
    x_ref, vec_ref, h1_ref, h2_ref, hid_ref, feat_ref, wink_ref, colk_ref, winv_ref, colv_ref, winm_ref, colm_ref,
    half_ref, tot_ref,
):
    own, ins, hid, feats, vecs, wide = z.own, z.ins, z.hid, z.feats, z.vecs, z.wide
    chunk = 2 * own
    for r in range(z.n_row):
        for k in range(3):
            lanes = pl.ds(k * wide + r * own, own)
            x_ref[:, lanes] = blocks_ref[r, k * z.part : k * z.part + ins]
            vec_ref[:, lanes] = blocks_ref[r, k * z.part + ins : (k + 1) * z.part]
    w_all = jnp.concatenate(
        [w_in_ref[...], b_in_ref[...], jnp.zeros((ins - z.depth - 1, hid), F32)], 0
    )
    w1, w2, w3 = split(w_all, 3)
    w_stack = stack([w1, w1, w2, w2, w1, w3])
    o1, o2 = split(w_out_ref[...])
    out_m = jnp.concatenate([o1, o2], 1).astype(BF)
    out_k = jnp.concatenate([o1, o1, o2, o2], 1).astype(BF)
    ones = jnp.ones((16, chunk), F32)

    def forward(i):
        lanes = pl.ds(i * chunk, chunk)
        x1, x2, x3 = split(x_ref[:, lanes], 3)
        h = jnp.tanh(mm_tn(w_stack, stack([x1, x2, x1, x2, x3, x1])))
        hid_ref[:, lanes] = h
        h1 = h.astype(BF)
        h2 = (h - h1.astype(F32)).astype(BF)
        h1_ref[:, lanes], h2_ref[:, lanes] = h1, h2
        raw = mm_tn(out_m, h1) + mm_tn(out_m, h2)
        feat_ref[:, lanes] = raw[:feats] + raw[feats:]

    each(z.total // chunk, forward)

    def window(i):
        lanes = pl.ds(i * chunk, chunk)
        f1, f2 = split(feat_ref[:, lanes])
        wink_ref[lanes, :] = stack([f1, f2, f1, f2]).T
        winm_ref[:, lanes] = stack([f1, f2, ones])
        s1, s2 = split(vec_ref[:, lanes])
        winv_ref[lanes, :] = stack([s1, s2, s1, s2]).T
        exact = f1 + f2
        half_ref[lanes, :] = mm_tn(stack(split(exact * exact, 3)), jnp.full((3 * feats, own), 0.5, BF))
        tot_ref[:, lanes] = jnp.zeros((tot_ref.shape[0], chunk), F32)

    each(wide // chunk, window)

    def columns(i):
        lanes = pl.ds(wide + i * chunk, chunk)
        f1, f2 = split(feat_ref[:, lanes])
        p1, p2 = split(vec_ref[:, lanes])
        exact = f1 + f2
        half = 0.5 * jnp.sum(exact * exact, 0, keepdims=True)
        f_stack, p_stack = stack([f1, f1, f2, f2]), stack([p1, p1, p2, p2])
        m_stack = stack([f1, f2, ones])

        def against(k, raw):
            rows = pl.ds(k * wide_step, wide_step)
            norm = half_ref[rows, :]
            norm = jnp.concatenate([norm] * (chunk // own), 1)
            kern = jnp.exp(mm(wink_ref[rows, :], f_stack) - norm - half)
            weigh = kern * mm(winv_ref[rows, :], p_stack)
            g1 = weigh.astype(BF)
            g2 = (weigh - g1.astype(F32)).astype(BF)
            m = winm_ref[:, rows]
            tot_ref[:, rows] += mm_nt(m_stack, g1) + mm_nt(m_stack, g2)
            return raw + mm(m, g1) + mm(m, g2)

        wide_step = min(wide, 512)
        raw = jnp.zeros((2 * feats + 16, chunk), F32)
        if wide == wide_step:
            raw = against(0, raw)
        else:
            raw = lax.fori_loop(0, wide // wide_step, against, raw)
        feat_ref[:, lanes] = raw[:feats] + raw[feats : 2 * feats] - exact * raw[2 * feats : 2 * feats + 1]

    each(2 * wide // chunk, columns)
    col_grad_ref[...] = feat_ref[:, wide : wide + own]

    def window_grad(i):
        lanes = pl.ds(i * chunk, chunk)
        f1, f2 = split(feat_ref[:, lanes])
        raw = tot_ref[:, lanes]
        feat_ref[:, lanes] = raw[:feats] + raw[feats : 2 * feats] - (f1 + f2) * raw[2 * feats : 2 * feats + 1]

    each(wide // chunk, window_grad)

    pack_ref[...] = jnp.zeros(pack_ref.shape, F32)

    def backward(i):
        lanes = pl.ds(i * chunk, chunk)
        t1, t2 = split(feat_ref[:, lanes])
        h = hid_ref[:, lanes]
        g = mm(out_k, stack([t1, t2, t1, t2])) * (1.0 - h * h)
        t_stack = stack([t1, t2])
        raw = mm_nt(t_stack, h1_ref[:, lanes]) + mm_nt(t_stack, h2_ref[:, lanes])
        pack_ref[:feats] += raw[:feats] + raw[feats:]
        x1, x2 = split(x_ref[:, lanes])
        x_stack = stack([x1, x2])
        g1 = g.astype(BF)
        g2 = (g - g1.astype(F32)).astype(BF)
        raw = mm_nt(x_stack, g1) + mm_nt(x_stack, g2)
        pack_ref[feats:] += raw[:ins] + raw[ins:]

    each(z.total // chunk, backward)


def finish_kernel(z, mine_ref, theirs_ref, grad_in_ref, grad_bias_ref, grad_out_ref):
    both = mine_ref[...] + theirs_ref[...]
    grad_out_ref[...] = both[: z.feats].T
    grad_in_ref[...] = both[z.feats : z.feats + z.depth]
    grad_bias_ref[...] = both[z.feats + z.depth : z.feats + z.depth + 1]


def whole(count):
    return [pl.BlockSpec(memory_space=VMEM)] * count


def body(n_row, n_col, protocols, w_in, b_in, w_out, solved, probes, window_blocks):
    z = Sizes(protocols.shape[0], solved.shape[0], w_out.shape[0], w_out.shape[1], protocols.shape[1], n_row)
    bits = bits_of(n_col)
    shared, joined = bits[:-1], bits[-1]
    blk = jax.ShapeDtypeStruct((z.part, z.own), F32)
    window, columns, apart = pl.pallas_call(
        functools.partial(prepare_kernel, z),
        out_shape=(blk, blk, jax.ShapeDtypeStruct((8, z.own), jnp.int32)),
        in_specs=[pl.BlockSpec(memory_space=pltpu.SMEM)] + whole(3),
        out_specs=tuple(whole(3)),
        compiler_params=pltpu.CompilerParams(vmem_limit_bytes=2 << 20),
        name="prepare",
    )(window_blocks, protocols, solved, probes)

    def nearer(bit, mine, theirs):
        return jnp.where((apart[:1] & bit) == 0, mine, theirs)

    for bit in shared:
        window = nearer(bit, window, swap(window, "col", n_col, bit))
    got = swap(jnp.concatenate([window, columns]), "col", n_col, joined)
    window = nearer(joined, window, got[: z.part])
    blocks = jnp.concatenate([window, columns, got[z.part :]])[None]
    for bit in reversed(bits_of(n_row)):
        blocks = jnp.concatenate([blocks, swap(blocks, "row", n_row, bit)])

    feats, total, wide = z.feats, z.total, z.wide
    col_grad, pack = pl.pallas_call(
        functools.partial(compute_kernel, z),
        out_shape=(jax.ShapeDtypeStruct((feats, z.own), F32), jax.ShapeDtypeStruct((feats + z.ins, z.hid), F32)),
        in_specs=whole(4),
        out_specs=tuple(whole(2)),
        scratch_shapes=[
            VMEM((z.ins, total), F32),
            VMEM((z.vecs, total), F32),
            VMEM((z.hid, total), BF),
            VMEM((z.hid, total), BF),
            VMEM((z.hid, total), F32),
            VMEM((feats, total), F32),
            VMEM((wide, 4 * feats), BF),
            VMEM((8, 128), BF),
            VMEM((wide, 4 * z.vecs), BF),
            VMEM((8, 128), BF),
            VMEM((2 * feats + 16, wide), BF),
            VMEM((8, 128), BF),
            VMEM((wide, z.own), F32),
            VMEM((2 * feats + 16, wide), F32),
        ],
        compiler_params=pltpu.CompilerParams(vmem_limit_bytes=48 << 20),
        name="compute",
    )(blocks, w_in, b_in.reshape(1, -1), w_out)

    for bit in reversed(shared[1:]):
        pack = pack + swap(pack, "col", n_col, bit)
    grad_in, grad_bias, grad_out = pl.pallas_call(
        functools.partial(finish_kernel, z),
        out_shape=(
            jax.ShapeDtypeStruct((z.depth, z.hid), F32),
            jax.ShapeDtypeStruct((1, z.hid), F32),
            jax.ShapeDtypeStruct((z.hid, feats), F32),
        ),
        in_specs=whole(2),
        out_specs=tuple(whole(3)),
        compiler_params=pltpu.CompilerParams(vmem_limit_bytes=2 << 20),
        name="finish",
    )(pack, swap(pack, "col", n_col, shared[0]))
    return (col_grad, grad_in, grad_bias.reshape(-1), grad_out)


def solution(mesh):
    n_row, n_col = mesh.shape["row"], mesh.shape["col"]
    cut = P(None, ("row", "col"))

    def per_device(*args):
        return body(n_row, n_col, *args)

    return jax.shard_map(
        per_device,
        mesh=mesh,
        in_specs=(cut, P(), P(), P(), cut, cut, P()),
        out_specs=(cut, P(), P(), P()),
        check_vma=False,
    )
```

```python
import functools

import jax
import jax.numpy as jnp
from jax import lax
from jax.experimental import pallas as pl
from jax.experimental.pallas import tpu as pltpu
from jax.sharding import PartitionSpec as P

BF, F32 = jnp.bfloat16, jnp.float32
VMEM = pltpu.VMEM


def swap(value, axis, size, bit):
    return lax.ppermute(value, axis, [(i, i ^ bit) for i in range(size)])


def bits_of(size):
    return [1 << k for k in range(size.bit_length() - 1)]


def split(value, terms=2):
    parts = []
    for _ in range(terms):
        part = value.astype(BF).astype(F32)
        parts.append(part)
        value = value - part
    return parts


def stack(parts):
    return jnp.concatenate(parts, 0).astype(BF)


def mm(a, b):
    return lax.dot_general(a, b, (((1,), (0,)), ((), ())), preferred_element_type=F32)


def mm_nt(a, b):
    return lax.dot_general(a, b, (((1,), (1,)), ((), ())), preferred_element_type=F32)


def mm_tn(a, b):
    return lax.dot_general(a, b, (((0,), (0,)), ((), ())), preferred_element_type=F32)


def each(count, step):
    if count <= 4:
        for i in range(count):
            step(i)
    else:
        lax.fori_loop(0, count, lambda i, c: (step(i), c)[1], 0)


def up(value, to):
    return -(-value // to) * to


class Sizes:
    def __init__(self, depth, vecs, hid, feats, own, n_row):
        self.depth, self.vecs, self.hid, self.feats, self.own = depth, vecs, hid, feats, own
        self.ins = up(depth + 1, 8)
        self.part = self.ins + vecs
        self.groups = n_row // 2
        self.wide = self.groups * own
        self.chunk = min(2 * own, self.wide)
        self.rows = 2 * feats + 16

    def half(self):
        w = self.wide
        return dict(
            x=((self.ins, 3 * w), F32),
            h1=((self.hid, 3 * w), BF),
            h2=((self.hid, 3 * w), BF),
            m=((self.rows, 3 * w), BF),
            vec=((4 * self.vecs, 2 * w), BF),
            norm=((8, 2 * w), F32),
            wink=((w, 4 * self.feats), BF),
            winv=((w, 4 * self.vecs), BF),
            winn=((w, self.own), F32),
        )

    def sums(self):
        return dict(raw=((self.rows, 2 * self.wide), F32), tot=((self.rows, self.wide), F32))


class Refs:
    def __init__(self, names, refs):
        self.__dict__.update(zip(names, refs, strict=True))


def prepare_kernel(z, blocks_hbm, in_hbm, vec_hbm, probes_hbm, window_ref, columns_ref, apart_ref, blocks, sems):
    depth, ins = z.depth, z.ins
    moves = (
        (blocks_hbm, blocks),
        (in_hbm, window_ref.at[:depth]),
        (vec_hbm, window_ref.at[ins:]),
        (probes_hbm, columns_ref.at[ins:]),
    )
    copies = [pltpu.make_async_copy(src, dst, sems.at[i]) for i, (src, dst) in enumerate(moves)]
    for copy in copies:
        copy.start()
    for copy in copies:
        copy.wait()
    ones = jnp.where(lax.broadcasted_iota(jnp.int32, (ins - depth, z.own), 0) == 0, 1.0, 0.0)
    window_ref[depth:ins] = ones
    columns_ref[:depth] = window_ref[:depth]
    columns_ref[depth:ins] = ones
    apart_ref[...] = jnp.full(apart_ref.shape, blocks[lax.axis_index("row")] ^ lax.axis_index("col"), jnp.int32)


def pick_kernel(z, own_ref, apart_ref, far_in, far_vec, window_ref):
    depth, ins = z.depth, z.ins

    def nearer(mine, theirs):
        return jnp.where(jnp.broadcast_to(apart_ref[:1] & 1, mine.shape) == 0, mine, theirs)

    window_ref[:depth] = nearer(own_ref[:depth], far_in[...])
    window_ref[depth:ins] = own_ref[depth:ins]
    window_ref[ins:] = nearer(own_ref[ins:], far_vec[...])


def weights_kernel(z, w_in, b_in, w_out, w_stack_ref, out_m_ref, out_k_ref):
    w_all = jnp.concatenate([w_in[0], b_in[...], jnp.zeros((z.ins - z.depth - 1, z.hid), F32)], 0)
    w1, w2, w3 = split(w_all, 3)
    w_stack_ref[...] = stack([w1, w1, w2, w2, w1, w3]).T
    o1, o2 = split(w_out[...])
    out_m_ref[...] = stack([o1, o2])
    out_k_ref[...] = stack([o1, o1, o2, o2]).T


def features(z, blocks_ref, w_stack, out_m, s):
    own, ins, feats, wide, chunk, part = z.own, z.ins, z.feats, z.wide, z.chunk, z.part
    per = chunk // own

    def source(i, start, count, third):
        return jnp.concatenate(
            [blocks_ref[i * per + r, third * part + start : third * part + start + count] for r in range(per)], 1
        )

    for third in range(3):

        def one(i, third=third):
            lanes = pl.ds(third * wide + i * chunk, chunk)
            x = source(i, 0, ins, third)
            s.x[:, lanes] = x
            x1, x2, x3 = split(x, 3)
            h = jnp.tanh(mm(w_stack, stack([x1, x2, x1, x2, x3, x1])))
            h1 = h.astype(BF)
            h2 = (h - h1.astype(F32)).astype(BF)
            s.h1[:, lanes], s.h2[:, lanes] = h1, h2
            raw = mm(out_m, h1) + mm(out_m, h2)
            f1, f2 = split(raw[:feats] + raw[feats:])
            s.m[:, lanes] = stack([f1, f2, jnp.ones((16, chunk), F32)])
            exact = f1 + f2
            square = exact * exact
            v1, v2 = split(source(i, ins, z.vecs, third))
            if third == 0:
                rows = pl.ds(i * chunk, chunk)
                s.wink[rows, :] = stack([f1, f2, f1, f2]).T
                s.winv[rows, :] = stack([v1, v2, v1, v2]).T
                s.winn[rows, :] = mm_tn(stack(split(square, 3)), jnp.full((3 * feats, own), 0.5, BF))
            else:
                here = pl.ds((third - 1) * wide + i * chunk, chunk)
                s.vec[:, here] = stack([v1, v1, v2, v2])
                s.norm[:, here] = jnp.broadcast_to(0.5 * jnp.sum(square, 0, keepdims=True), (8, chunk))

        each(wide // chunk, one)


def tiles(z, win, col, raw_ref, tot_ref):
    feats, wide, chunk = z.feats, z.wide, z.chunk

    def columns(i):
        here, lanes = pl.ds(i * chunk, chunk), pl.ds(wide + i * chunk, chunk)
        m = col.m[:, lanes]
        f1, f2 = m[:feats], m[feats : 2 * feats]
        f_stack = jnp.concatenate([f1, f1, f2, f2], 0)
        vec, norm = col.vec[:, here], col.norm[:1, here]

        def windows(k):
            rows = pl.ds(k * chunk, chunk)
            far = jnp.concatenate([win.winn[rows, :]] * (chunk // z.own), 1)
            kern = jnp.exp(mm(win.wink[rows, :], f_stack) - far - norm)
            weigh = kern * mm(win.winv[rows, :], vec)
            g1 = weigh.astype(BF)
            g2 = (weigh - g1.astype(F32)).astype(BF)
            mine = win.m[:, rows]
            tot_ref[:, rows] += mm_nt(m, g1) + mm_nt(m, g2)
            raw_ref[:, here] += mm(mine, g1) + mm(mine, g2)

        each(wide // chunk, windows)

    each(2 * wide // chunk, columns)


def early_kernel(z, names, blocks_ref, w_stack_ref, out_m_ref, *outs):
    s = Refs(names, outs)
    features(z, blocks_ref, w_stack_ref[...], out_m_ref[...], s)
    s.raw[...] = jnp.zeros(s.raw.shape, F32)
    s.tot[...] = jnp.zeros(s.tot.shape, F32)
    tiles(z, s, s, s.raw, s.tot)


def late_kernel(z, names, blocks_ref, w_stack_ref, out_m_ref, out_k_ref, *refs):
    feats, wide, chunk, ins = z.feats, z.wide, z.chunk, z.ins
    n = len(names)
    a, (col_grad_ref, pack_ref), b = Refs(names, refs[:n]), refs[n : n + 2], Refs(names, refs[n + 2 : 2 * n + 2])
    raw_ref, tot_ref, grad_ref = refs[2 * n + 2 :]
    features(z, blocks_ref, w_stack_ref[...], out_m_ref[...], b)
    raw_ref[...] = a.raw[...]
    tot_ref[...] = a.tot[...]
    b.raw[...] = jnp.zeros(b.raw.shape, F32)
    b.tot[...] = jnp.zeros(b.tot.shape, F32)
    tiles(z, b, a, raw_ref, b.tot)
    tiles(z, a, b, b.raw, tot_ref)
    tiles(z, b, b, b.raw, b.tot)
    pack_ref[...] = jnp.zeros(pack_ref.shape, F32)
    out_k = out_k_ref[...]
    for k, (s, raw, tot) in enumerate(((a, raw_ref, tot_ref), (b, b.raw, b.tot))):

        def backward(i, s=s, source=None, start=0, shift=0, first=False):
            lanes = pl.ds(start + i * chunk, chunk)
            sums = source[:, pl.ds(i * chunk + shift, chunk)]
            m = s.m[:, lanes].astype(F32)
            exact = m[:feats] + m[feats : 2 * feats]
            t = sums[:feats] + sums[feats : 2 * feats] - exact * sums[2 * feats : 2 * feats + 1]
            if first:
                grad_ref[:, pl.ds(i * chunk, chunk)] = t
            t1, t2 = split(t)
            h1, h2 = s.h1[:, lanes], s.h2[:, lanes]
            h = h1.astype(F32) + h2.astype(F32)
            g = mm(out_k, stack([t1, t2, t1, t2])) * (1.0 - h * h)
            t_stack = stack([t1, t2])
            both = mm_nt(t_stack, h1) + mm_nt(t_stack, h2)
            pack_ref[:feats] += both[:feats] + both[feats:]
            x1, x2 = split(s.x[:, lanes])
            x_stack = stack([x1, x2])
            g1 = g.astype(BF)
            g2 = (g - g1.astype(F32)).astype(BF)
            both = mm_nt(x_stack, g1) + mm_nt(x_stack, g2)
            pack_ref[feats:] += both[:ins] + both[ins:]

        each(2 * wide // chunk, functools.partial(backward, source=raw, start=wide, first=k == 0))
        each(wide // chunk, functools.partial(backward, source=tot))
    col_grad_ref[...] = grad_ref[:, : z.own]


def finish_kernel(z, mine_ref, theirs_ref, grad_in_ref, grad_bias_ref, grad_out_ref):
    both = mine_ref[...] + theirs_ref[...]
    grad_out_ref[...] = both[: z.feats]
    grad_in_ref[...] = both[z.feats : z.feats + z.depth]
    grad_bias_ref[...] = both[z.feats + z.depth : z.feats + z.depth + 1]


def whole(count):
    return [pl.BlockSpec(memory_space=VMEM)] * count


def shapes(spec):
    return [jax.ShapeDtypeStruct(*v) for v in spec.values()]


def call(kernel, name, outs, operands, scratch=(), limit=4, cost=1, place=VMEM):
    return pl.pallas_call(
        kernel,
        out_shape=tuple(outs),
        in_specs=[pl.BlockSpec(memory_space=place)] * len(operands),
        out_specs=tuple(whole(len(outs))),
        scratch_shapes=list(scratch),
        compiler_params=pltpu.CompilerParams(vmem_limit_bytes=limit << 20),
        cost_estimate=pl.CostEstimate(flops=cost * 10**8, bytes_accessed=10**6, transcendentals=0),
        name=name,
    )(*operands)


def body(n_row, n_col, protocols, w_in, b_in, w_out, solved, probes, window_blocks):
    depth, own = protocols.shape
    z = Sizes(depth, solved.shape[0], w_out.shape[0], w_out.shape[1], own, n_row)
    bits = bits_of(n_col)
    shared, joined = bits[:-1], bits[-1]
    limit = 12 if n_row <= 4 else 48
    f32 = functools.partial(jax.ShapeDtypeStruct, dtype=F32)

    theirs = swap(protocols, "col", n_col, 1), swap(solved, "col", n_col, 1)
    blk = f32((z.part, own))
    window, columns, apart = call(
        functools.partial(prepare_kernel, z),
        "prepare",
        (blk, blk, jax.ShapeDtypeStruct((8, own), jnp.int32)),
        [pltpu.with_memory_space_constraint(v, pltpu.HBM) for v in (window_blocks, protocols, solved, probes)],
        [pltpu.SMEM(window_blocks.shape, jnp.int32), pltpu.SemaphoreType.DMA((4,))],
        place=pltpu.HBM,
    )
    (window,) = call(functools.partial(pick_kernel, z), "pick", (blk,), (window, apart, *theirs))

    def nearer(bit, mine, theirs):
        return jnp.where((apart[:1] & bit) == 0, mine, theirs)

    window, w_in, b_in, w_out = lax.optimization_barrier((window, w_in, b_in, w_out))
    w_stack, out_m, out_k = call(
        functools.partial(weights_kernel, z),
        "weights",
        (
            jax.ShapeDtypeStruct((z.hid, 6 * z.ins), BF),
            jax.ShapeDtypeStruct((2 * z.feats, z.hid), BF),
            jax.ShapeDtypeStruct((z.hid, 4 * z.feats), BF),
        ),
        (w_in[None], b_in.reshape(1, -1), w_out.T),
    )
    for bit in shared[1:]:
        window = nearer(bit, window, swap(window, "col", n_col, bit))
    window, w_stack, out_m, out_k = lax.optimization_barrier((window, w_stack, out_m, out_k))
    got = swap(jnp.concatenate([window, columns]), "col", n_col, joined)
    window = nearer(joined, window, got[: z.part])
    blocks = jnp.concatenate([window, columns, got[z.part :]])[None]
    for bit in reversed(bits_of(n_row)[1:]):
        blocks = jnp.concatenate([blocks, swap(blocks, "row", n_row, bit)])
    far_blocks = swap(blocks, "row", n_row, 1)

    kept = z.half() | z.sums()
    early = call(
        functools.partial(early_kernel, z, list(kept)),
        "early",
        shapes(kept),
        (blocks, w_stack, out_m),
        limit=limit,
        cost=10,
    )
    col_grad, pack = call(
        functools.partial(late_kernel, z, list(kept)),
        "late",
        (f32((z.feats, own)), f32((z.feats + z.ins, z.hid))),
        (far_blocks, w_stack, out_m, out_k, *early),
        [VMEM(*v) for v in (kept | {"r": kept["raw"], "t": kept["tot"], "g": ((z.feats, 2 * z.wide), F32)}).values()],
        limit=limit,
        cost=20,
    )
    for bit in reversed(shared[1:]):
        pack = pack + swap(pack, "col", n_col, bit)
    grad_in, grad_bias, grad_out = call(
        functools.partial(finish_kernel, z),
        "finish",
        (f32((depth, z.hid)), f32((1, z.hid)), f32((z.feats, z.hid))),
        (pack, swap(pack, "col", n_col, shared[0])),
    )
    return (col_grad, grad_in, grad_bias.reshape(-1), grad_out.T)


def solution(mesh):
    n_row, n_col = mesh.shape["row"], mesh.shape["col"]
    cut = P(None, ("row", "col"))

    def per_device(*args):
        return body(n_row, n_col, *args)

    return jax.shard_map(
        per_device,
        mesh=mesh,
        in_specs=(cut, P(), P(), P(), cut, cut, P()),
        out_specs=(cut, P(), P(), P()),
        check_vma=False,
    )
```

```python
import functools

import jax
import jax.numpy as jnp
from jax import lax
from jax.experimental import pallas as pl
from jax.experimental.pallas import tpu as pltpu
from jax.sharding import PartitionSpec as P

BF, F32 = jnp.bfloat16, jnp.float32
VMEM = pltpu.VMEM


def swap(value, axis, size, bit):
    return lax.ppermute(value, axis, [(i, i ^ bit) for i in range(size)])


def bits_of(size):
    return [1 << k for k in range(size.bit_length() - 1)]


def split(value, terms=2):
    parts = []
    for _ in range(terms):
        part = value.astype(BF).astype(F32)
        parts.append(part)
        value = value - part
    return parts


def stack(parts):
    return jnp.concatenate(parts, 0).astype(BF)


def mm(a, b):
    return lax.dot_general(a, b, (((1,), (0,)), ((), ())), preferred_element_type=F32)


def mm_nt(a, b):
    return lax.dot_general(a, b, (((1,), (1,)), ((), ())), preferred_element_type=F32)


def mm_tn(a, b):
    return lax.dot_general(a, b, (((0,), (0,)), ((), ())), preferred_element_type=F32)


def each(count, step):
    if count <= 4:
        for i in range(count):
            step(i)
    else:
        lax.fori_loop(0, count, lambda i, c: (step(i), c)[1], 0)


def flow(count, *stages):
    held = {}
    for t in range(count + len(stages) - 1):
        for depth, stage in enumerate(stages):
            k = t - depth
            if 0 <= k < count:
                held[k] = stage(k, held.get(k))


def up(value, to):
    return -(-value // to) * to


class Sizes:
    def __init__(self, depth, vecs, hid, feats, own, n_row):
        self.depth, self.vecs, self.hid, self.feats, self.own = depth, vecs, hid, feats, own
        self.ins = up(depth + 1, 8)
        self.part = self.ins + vecs
        self.wide = n_row // 2 * own
        self.cols = n_row * own
        self.rows = 2 * feats + 16
        self.win_step = min(256, self.wide)
        self.win_piece = min(256, self.win_step)
        self.col_step = min(512, self.cols)

    def network(self, lanes):
        return dict(
            x=((self.ins, lanes), F32),
            h1=((self.hid, lanes), BF),
            h2=((self.hid, lanes), BF),
            m=((self.rows, lanes), BF),
        )

    def windows(self):
        w = self.wide
        return self.network(w) | dict(
            key=((w, 4 * self.feats), BF),
            vec=((w, 4 * self.vecs), BF),
            norm=((w, self.own), F32),
            sums=((w, self.rows), F32),
        )

    def columns(self):
        c = self.cols
        return self.network(c) | dict(vec=((4 * self.vecs, c), BF), norm=((8, c), F32), sums=((self.rows, c), F32))


class Refs:
    def __init__(self, names, refs):
        self.__dict__.update(zip(names, refs, strict=True))


def prepare_kernel(z, blocks_hbm, in_hbm, vec_hbm, probes_hbm, window_ref, columns_ref, apart_ref, blocks, sems):
    depth, ins = z.depth, z.ins
    moves = (
        (blocks_hbm, blocks),
        (in_hbm, window_ref.at[:depth]),
        (vec_hbm, window_ref.at[ins:]),
        (probes_hbm, columns_ref.at[ins:]),
    )
    copies = [pltpu.make_async_copy(src, dst, sems.at[i]) for i, (src, dst) in enumerate(moves)]
    for copy in copies:
        copy.start()
    for copy in copies:
        copy.wait()
    ones = jnp.where(lax.broadcasted_iota(jnp.int32, (ins - depth, z.own), 0) == 0, 1.0, 0.0)
    window_ref[depth:ins] = ones
    columns_ref[:depth] = window_ref[:depth]
    columns_ref[depth:ins] = ones
    apart_ref[...] = jnp.full(apart_ref.shape, blocks[lax.axis_index("row")] ^ lax.axis_index("col"), jnp.int32)


def pick_kernel(z, own_ref, apart_ref, far_in, far_vec, window_ref):
    depth, ins = z.depth, z.ins

    def nearer(mine, theirs):
        return jnp.where(jnp.broadcast_to(apart_ref[:1] & 1, mine.shape) == 0, mine, theirs)

    window_ref[:depth] = nearer(own_ref[:depth], far_in[...])
    window_ref[depth:ins] = own_ref[depth:ins]
    window_ref[ins:] = nearer(own_ref[ins:], far_vec[...])


def weights_kernel(z, w_in, b_in, w_out, w_stack_ref, out_m_ref, out_k_ref):
    w_all = jnp.concatenate([w_in[0], b_in[...], jnp.zeros((z.ins - z.depth - 1, z.hid), F32)], 0)
    w1, w2, w3 = split(w_all, 3)
    w_stack_ref[...] = stack([w1, w1, w2, w2, w1, w3]).T
    o1, o2 = split(w_out[...])
    out_m_ref[...] = stack([o1, o2])
    out_k_ref[...] = stack([o1, o1, o2, o2]).T


def network(z, s, w_stack, out_m):
    def into(lanes):
        x1, x2, x3 = split(s.x[:, lanes], 3)
        return mm(w_stack, stack([x1, x2, x1, x2, x3, x1]))

    def middle(lanes, pre):
        h = jnp.tanh(pre)
        h1 = h.astype(BF)
        h2 = (h - h1.astype(F32)).astype(BF)
        s.h1[:, lanes], s.h2[:, lanes] = h1, h2
        return mm(out_m, h1) + mm(out_m, h2)

    def out(lanes, raw):
        f1, f2 = split(raw[: z.feats] + raw[z.feats :])
        s.m[:, lanes] = stack([f1, f2, jnp.ones((16, raw.shape[1]), F32)])
        exact = f1 + f2
        return 0.5 * jnp.sum(exact * exact, 0, keepdims=True)

    return into, middle, out


def window_features(z, blocks_ref, s, w_stack, out_m):
    own, part, step = z.own, z.part, z.win_step
    for r in range(z.wide // own):
        here = pl.ds(r * own, own)
        s.x[:, here] = blocks_ref[r * part : r * part + z.ins]
        v1, v2 = split(blocks_ref[r * part + z.ins : (r + 1) * part])
        s.vec[here, :] = stack([v1, v2, v1, v2]).T
    into, middle, out = network(z, s, w_stack, out_m)

    def one(i):
        rows = [pl.ds(i * step + k * z.win_piece, z.win_piece) for k in range(step // z.win_piece)]

        def last(k, raw):
            norm = out(rows[k], raw)
            s.key[rows[k], :] = jnp.concatenate([s.m[: 2 * z.feats, rows[k]]] * 2, 0).T
            s.norm[rows[k], :] = jnp.broadcast_to(norm, (own, z.win_piece)).T

        flow(len(rows), lambda k, _: into(rows[k]), lambda k, pre: middle(rows[k], pre), last)

    each(z.wide // step, one)
    s.sums[...] = jnp.zeros(s.sums.shape, F32)


def column_blocks(z, blocks_ref, s):
    for r in range(z.cols // z.own):
        here = pl.ds(r * z.own, z.own)
        s.x[:, here] = blocks_ref[r * z.part : r * z.part + z.ins]
        v1, v2 = split(blocks_ref[r * z.part + z.ins : (r + 1) * z.part])
        s.vec[:, here] = stack([v1, v1, v2, v2])


def beside(parts):
    return jnp.concatenate(parts, 1)


def tile(z, win, col):
    feats, step = z.feats, z.win_step
    single = z.wide == step

    def products(lanes, rows):
        m = col.m[: 2 * feats, lanes]
        f1, f2 = m[:feats], m[feats:]
        cross = mm(win.key[rows, :], jnp.concatenate([f1, f1, f2, f2], 0))
        return cross, mm(win.vec[rows, :], col.vec[:, lanes])

    def weighed(lanes, rows, dots):
        far = beside([win.norm[rows, :]] * (z.col_step // z.own))
        weigh = jnp.exp(dots[0] - far - col.norm[:1, lanes]) * dots[1]
        g1 = weigh.astype(BF)
        g2 = (weigh - g1.astype(F32)).astype(BF)
        both = jnp.concatenate([g1, g2], 0)
        mine = win.m[:, rows]
        part = mm_nt(both, col.m[:, lanes])
        win.sums[rows, :] += part[:step] + part[step:]
        return mm(beside([mine, mine]), both)

    def first(lanes):
        return products(lanes, pl.ds(0, step)) if single else None

    def second(lanes, dots):
        if single:
            return weighed(lanes, pl.ds(0, step), dots)

        def add(k, sums):
            rows = pl.ds(k * step, step)
            return sums + weighed(lanes, rows, products(lanes, rows))

        return lax.fori_loop(0, z.wide // step, add, jnp.zeros((z.rows, z.col_step), F32))

    return first, second


def total_of(z, m, sums):
    feats = z.feats
    m = m[: 2 * feats].astype(F32)
    return sums[:feats] + sums[feats : 2 * feats] - (m[:feats] + m[feats:]) * sums[2 * feats : 2 * feats + 1]


def backprop(z, s, out_k, pack_ref):
    def first(lanes, total):
        t1, t2 = split(total)
        t_stack = stack([t1, t2])
        g = mm(out_k, jnp.concatenate([t_stack, t_stack], 0))
        both = mm_nt(beside([t_stack, t_stack]), beside([s.h1[:, lanes], s.h2[:, lanes]]))
        pack_ref[: z.feats] += both[: z.feats] + both[z.feats :]
        return g

    def second(lanes, g):
        h = s.h1[:, lanes].astype(F32) + s.h2[:, lanes].astype(F32)
        g = g * (1.0 - h * h)
        x_stack = stack(split(s.x[:, lanes]))
        g1 = g.astype(BF)
        g2 = (g - g1.astype(F32)).astype(BF)
        both = mm_nt(beside([x_stack, x_stack]), beside([g1, g2]))
        pack_ref[z.feats :] += both[: z.ins] + both[z.ins :]

    return first, second


def window_total(z, s, rows):
    return total_of(z, s.m[:, rows], s.sums[rows, :].T)


def window_backprop(z, s, out_k, pack_ref):
    first, second = backprop(z, s, out_k, pack_ref)

    def one(i):
        rows = pl.ds(i * z.win_step, z.win_step)
        second(rows, first(rows, window_total(z, s, rows)))

    each(z.wide // z.win_step, one)


def column_steps(z):
    return [pl.ds(k * z.col_step, z.col_step) for k in range(z.cols // z.col_step)]


def column_features(z, blocks_ref, col, win, w_stack, out_m):
    column_blocks(z, blocks_ref, col)
    into, middle, out = network(z, col, w_stack, out_m)
    first, second = tile(z, win, col)
    lanes = column_steps(z)

    def third(k, raw):
        col.norm[:, lanes[k]] = jnp.broadcast_to(out(lanes[k], raw), (8, z.col_step))
        return first(lanes[k])

    def fourth(k, dots):
        col.sums[:, lanes[k]] = second(lanes[k], dots)

    flow(len(lanes), lambda k, _: into(lanes[k]), lambda k, pre: middle(lanes[k], pre), third, fourth)


def near_kernel(z, windows_ref, columns_ref, w_stack_ref, out_m_ref, *refs):
    n = len(z.windows())
    win, col = Refs(z.windows(), refs[:n]), Refs(z.columns(), refs[n:])
    w_stack, out_m = w_stack_ref[...], out_m_ref[...]
    window_features(z, windows_ref, win, w_stack, out_m)
    column_features(z, columns_ref, col, win, w_stack, out_m)


def far_kernel(z, columns_ref, w_stack_ref, out_m_ref, out_k_ref, *refs):
    n, c = len(z.windows()), len(z.columns())
    win, col = Refs(z.windows(), refs[:n]), Refs(z.columns(), refs[n : n + c])
    pack_ref, sums_ref = refs[n + c :]
    sums_ref[...] = win.sums[...]
    win.sums = sums_ref
    column_features(z, columns_ref, col, win, w_stack_ref[...], out_m_ref[...])
    pack_ref[...] = jnp.zeros(pack_ref.shape, F32)
    window_backprop(z, win, out_k_ref[...], pack_ref)


def late_kernel(z, windows_ref, w_stack_ref, out_m_ref, out_k_ref, *refs):
    c = len(z.columns())
    cols = [Refs(z.columns(), refs[:c]), Refs(z.columns(), refs[c : 2 * c])]
    early_pack_ref, col_grad_ref, pack_ref = refs[2 * c : 2 * c + 3]
    win = Refs(z.windows(), refs[2 * c + 3 :])
    pack_ref[...] = early_pack_ref[...]
    window_features(z, windows_ref, win, w_stack_ref[...], out_m_ref[...])
    out_k = out_k_ref[...]
    work = [(col, lanes) for col in cols for lanes in column_steps(z)]
    totals = []

    def total(k, dots):
        col, lanes = work[k]
        sums = col.sums[:, lanes] + tile(z, win, col)[1](lanes, dots)
        totals.append(total_of(z, col.m[:, lanes], sums))

    flow(len(work), lambda k, _: tile(z, win, work[k][0])[0](work[k][1]), total)
    col_grad_ref[...] = totals[0][:, : z.own]
    for i in range(z.wide // z.win_step):
        rows = pl.ds(i * z.win_step, z.win_step)
        work.append((win, rows))
        totals.append(window_total(z, win, rows))
    stages = [backprop(z, s, out_k, pack_ref) for s, _ in work]
    flow(len(work), lambda k, _: stages[k][0](work[k][1], totals[k]), lambda k, g: stages[k][1](work[k][1], g))


def finish_kernel(z, mine_ref, theirs_ref, own_ref, col_grad_ref, grad_in_ref, grad_bias_ref, grad_out_ref):
    col_grad_ref[...] = own_ref[...]
    both = mine_ref[...] + theirs_ref[...]
    grad_out_ref[...] = both[: z.feats]
    grad_in_ref[...] = both[z.feats : z.feats + z.depth]
    grad_bias_ref[...] = both[z.feats + z.depth : z.feats + z.depth + 1]


def whole(count):
    return [pl.BlockSpec(memory_space=VMEM)] * count


def shapes(spec):
    return [jax.ShapeDtypeStruct(*v) for v in spec.values()]


def call(kernel, name, outs, operands, scratch=(), limit=4, cost=1, place=VMEM):
    return pl.pallas_call(
        kernel,
        out_shape=tuple(outs),
        in_specs=[pl.BlockSpec(memory_space=place)] * len(operands),
        out_specs=tuple(whole(len(outs))),
        scratch_shapes=list(scratch),
        compiler_params=pltpu.CompilerParams(vmem_limit_bytes=limit << 20),
        cost_estimate=pl.CostEstimate(flops=cost * 10**8, bytes_accessed=10**6, transcendentals=0),
        name=name,
    )(*operands)


def body(n_row, n_col, protocols, w_in, b_in, w_out, solved, probes, window_blocks):
    depth, own = protocols.shape
    z = Sizes(depth, solved.shape[0], w_out.shape[0], w_out.shape[1], own, n_row)
    bits = bits_of(n_col)
    shared, joined = bits[:-1], bits[-1]
    limit = 12 if n_row <= 4 else 48
    f32 = functools.partial(jax.ShapeDtypeStruct, dtype=F32)

    theirs = swap(protocols, "col", n_col, 1), swap(solved, "col", n_col, 1)
    blk = f32((z.part, own))
    window, columns, apart = call(
        functools.partial(prepare_kernel, z),
        "prepare",
        (blk, blk, jax.ShapeDtypeStruct((8, own), jnp.int32)),
        [pltpu.with_memory_space_constraint(v, pltpu.HBM) for v in (window_blocks, protocols, solved, probes)],
        [pltpu.SMEM(window_blocks.shape, jnp.int32), pltpu.SemaphoreType.DMA((4,))],
        place=pltpu.HBM,
    )
    (window,) = call(functools.partial(pick_kernel, z), "pick", (blk,), (window, apart, *theirs))

    def nearer(bit, mine, theirs):
        return jnp.where((apart[:1] & bit) == 0, mine, theirs)

    window, w_in, b_in, w_out = lax.optimization_barrier((window, w_in, b_in, w_out))
    w_stack, out_m, out_k = call(
        functools.partial(weights_kernel, z),
        "weights",
        (
            jax.ShapeDtypeStruct((z.hid, 6 * z.ins), BF),
            jax.ShapeDtypeStruct((2 * z.feats, z.hid), BF),
            jax.ShapeDtypeStruct((z.hid, 4 * z.feats), BF),
        ),
        (w_in[None], b_in.reshape(1, -1), w_out.T),
    )
    for bit in shared[1:]:
        window = nearer(bit, window, swap(window, "col", n_col, bit))
    columns = jnp.concatenate([columns, swap(columns, "col", n_col, joined)])
    window, columns, w_stack, out_m, out_k = lax.optimization_barrier((window, columns, w_stack, out_m, out_k))
    for bit in reversed(bits_of(n_row)[1:]):
        columns = jnp.concatenate([columns, swap(columns, "row", n_row, bit)])
    far_columns = swap(columns, "row", n_row, 1)
    window = nearer(joined, window, swap(window, "col", n_col, joined))
    for bit in reversed(bits_of(n_row)[1:]):
        window = jnp.concatenate([window, swap(window, "row", n_row, bit)])
    far_window = swap(window, "row", n_row, 1)

    pack_shape = f32((z.feats + z.ins, z.hid))
    near = call(
        functools.partial(near_kernel, z),
        "near",
        (*shapes(z.windows()), *shapes(z.columns())),
        (window, columns, w_stack, out_m),
        limit=limit,
        cost=10,
    )
    windows, near = near[: len(z.windows())], near[len(z.windows()) :]
    *far, early_pack = call(
        functools.partial(far_kernel, z),
        "far",
        (*shapes(z.columns()), pack_shape),
        (far_columns, w_stack, out_m, out_k, *windows),
        [VMEM(*z.windows()["sums"])],
        limit=limit,
        cost=10,
    )
    col_grad, pack = call(
        functools.partial(late_kernel, z),
        "late",
        (f32((z.feats, own)), pack_shape),
        (far_window, w_stack, out_m, out_k, *near, *far, early_pack),
        [VMEM(*v) for v in z.windows().values()],
        limit=limit,
        cost=20,
    )
    for bit in reversed(shared[1:]):
        pack = pack + swap(pack, "col", n_col, bit)
    col_grad, grad_in, grad_bias, grad_out = call(
        functools.partial(finish_kernel, z),
        "finish",
        (f32((z.feats, own)), f32((depth, z.hid)), f32((1, z.hid)), f32((z.feats, z.hid))),
        (pack, swap(pack, "col", n_col, shared[0]), col_grad),
    )
    return (col_grad, grad_in, grad_bias.reshape(-1), grad_out.T)


def solution(mesh):
    n_row, n_col = mesh.shape["row"], mesh.shape["col"]
    cut = P(None, ("row", "col"))

    def per_device(*args):
        return body(n_row, n_col, *args)

    return jax.shard_map(
        per_device,
        mesh=mesh,
        in_specs=(cut, P(), P(), P(), cut, cut, P()),
        out_specs=(cut, P(), P(), P()),
        check_vma=False,
    )
```

```python
import functools

import jax
import jax.numpy as jnp
from jax import lax
from jax.experimental import pallas as pl
from jax.experimental.pallas import tpu as pltpu
from jax.sharding import PartitionSpec as P

BF, F32 = jnp.bfloat16, jnp.float32
VMEM = pltpu.VMEM


def swap(value, axis, size, bit):
    return lax.ppermute(value, axis, [(i, i ^ bit) for i in range(size)])


def bits_of(size):
    return [1 << k for k in range(size.bit_length() - 1)]


def split(value, terms=2):
    parts = []
    for _ in range(terms):
        part = value.astype(BF).astype(F32)
        parts.append(part)
        value = value - part
    return parts


def stack(parts):
    return jnp.concatenate(parts, 0).astype(BF)


def mm(a, b):
    return lax.dot_general(a, b, (((1,), (0,)), ((), ())), preferred_element_type=F32)


def mm_nt(a, b):
    return lax.dot_general(a, b, (((1,), (1,)), ((), ())), preferred_element_type=F32)


def mm_tn(a, b):
    return lax.dot_general(a, b, (((0,), (0,)), ((), ())), preferred_element_type=F32)


def each(count, step):
    if count <= 4:
        for i in range(count):
            step(i)
    else:
        lax.fori_loop(0, count, lambda i, c: (step(i), c)[1], 0)


def flow(count, *stages):
    held = {}
    for t in range(count + len(stages) - 1):
        for depth, stage in enumerate(stages):
            k = t - depth
            if 0 <= k < count:
                held[k] = stage(k, held.get(k))


def up(value, to):
    return -(-value // to) * to


class Sizes:
    def __init__(self, depth, vecs, hid, feats, own, n_row):
        self.depth, self.vecs, self.hid, self.feats, self.own = depth, vecs, hid, feats, own
        self.ins = up(depth + 1, 8)
        self.part = self.ins + vecs
        self.wide = n_row // 2 * own
        self.cols = n_row * own
        self.rows = 2 * feats + 16
        self.win_step = min(256, self.wide)
        self.col_step = min(512, self.cols)
        self.early_step = min(256, self.cols)

    def network(self, lanes):
        return dict(
            x=((self.ins, lanes), F32),
            h1=((self.hid, lanes), BF),
            h2=((self.hid, lanes), BF),
            m=((self.rows, lanes), BF),
        )

    def windows(self):
        w = self.wide
        return self.network(w) | dict(
            key=((w, 4 * self.feats), BF),
            vec=((w, 4 * self.vecs), BF),
            norm=((w, self.own), F32),
            sums=((w, self.rows), F32),
        )

    def columns(self):
        c = self.cols
        return self.network(c) | dict(vec=((4 * self.vecs, c), BF), norm=((8, c), F32), sums=((self.rows, c), F32))


class Refs:
    def __init__(self, names, refs):
        self.__dict__.update(zip(names, refs, strict=True))


def prepare_kernel(z, blocks_hbm, in_hbm, vec_hbm, probes_hbm, window_ref, columns_ref, apart_ref, blocks, sems):
    depth, ins = z.depth, z.ins
    moves = (
        (blocks_hbm, blocks),
        (in_hbm, window_ref.at[:depth]),
        (vec_hbm, window_ref.at[ins:]),
        (probes_hbm, columns_ref.at[ins:]),
    )
    copies = [pltpu.make_async_copy(src, dst, sems.at[i]) for i, (src, dst) in enumerate(moves)]
    for copy in copies:
        copy.start()
    for copy in copies:
        copy.wait()
    ones = jnp.where(lax.broadcasted_iota(jnp.int32, (ins - depth, z.own), 0) == 0, 1.0, 0.0)
    window_ref[depth:ins] = ones
    columns_ref[:depth] = window_ref[:depth]
    columns_ref[depth:ins] = ones
    apart_ref[...] = jnp.full(apart_ref.shape, blocks[lax.axis_index("row")] ^ lax.axis_index("col"), jnp.int32)


def pick_kernel(z, own_ref, apart_ref, far_in, far_vec, window_ref):
    depth, ins = z.depth, z.ins

    def nearer(mine, theirs):
        return jnp.where(jnp.broadcast_to(apart_ref[:1] & 1, mine.shape) == 0, mine, theirs)

    window_ref[:depth] = nearer(own_ref[:depth], far_in[...])
    window_ref[depth:ins] = own_ref[depth:ins]
    window_ref[ins:] = nearer(own_ref[ins:], far_vec[...])


def weights_kernel(z, w_in, b_in, w_out, w_stack_ref, out_m_ref, out_k_ref):
    w_all = jnp.concatenate([w_in[0], b_in[...], jnp.zeros((z.ins - z.depth - 1, z.hid), F32)], 0)
    w1, w2, w3 = split(w_all, 3)
    w_stack_ref[...] = stack([w1, w1, w2, w2, w1, w3]).T
    o1, o2 = split(w_out[...])
    out_m_ref[...] = stack([o1, o2])
    out_k_ref[...] = stack([o1, o1, o2, o2]).T


def network(z, s, w_stack, out_m):
    def into(lanes):
        x1, x2, x3 = split(s.x[:, lanes], 3)
        return mm(w_stack, stack([x1, x2, x1, x2, x3, x1]))

    def middle(lanes, pre):
        h = jnp.tanh(pre)
        h1 = h.astype(BF)
        h2 = (h - h1.astype(F32)).astype(BF)
        s.h1[:, lanes], s.h2[:, lanes] = h1, h2
        return mm(out_m, h1) + mm(out_m, h2)

    def out(lanes, raw):
        f1, f2 = split(raw[: z.feats] + raw[z.feats :])
        s.m[:, lanes] = stack([f1, f2, jnp.ones((16, raw.shape[1]), F32)])
        exact = f1 + f2
        return 0.5 * jnp.sum(exact * exact, 0, keepdims=True)

    return into, middle, out


def window_features(z, blocks_ref, s, w_stack, out_m, others=()):
    own, part, step = z.own, z.part, z.win_step
    for r in range(z.wide // own):
        here = pl.ds(r * own, own)
        s.x[:, here] = blocks_ref[r * part : r * part + z.ins]
        v1, v2 = split(blocks_ref[r * part + z.ins : (r + 1) * part])
        s.vec[here, :] = stack([v1, v2, v1, v2]).T
    into, middle, out = network(z, s, w_stack, out_m)
    for i in range(z.wide // step):
        rows = pl.ds(i * step, step)
        value = into(rows)
        other = others[i][0]() if others else None
        value = middle(rows, value)
        if others:
            others[i][1](other)
        norm = out(rows, value)
        s.key[rows, :] = jnp.concatenate([s.m[: 2 * z.feats, rows]] * 2, 0).T
        s.norm[rows, :] = jnp.broadcast_to(norm, (own, step)).T
    s.sums[...] = jnp.zeros(s.sums.shape, F32)


def column_blocks(z, blocks_ref, s):
    for r in range(z.cols // z.own):
        here = pl.ds(r * z.own, z.own)
        s.x[:, here] = blocks_ref[r * z.part : r * z.part + z.ins]
        v1, v2 = split(blocks_ref[r * z.part + z.ins : (r + 1) * z.part])
        s.vec[:, here] = stack([v1, v1, v2, v2])


def beside(parts):
    return jnp.concatenate(parts, 1)


def tile(z, win, col, width):
    feats, step = z.feats, z.win_step
    single = z.wide == step

    def products(lanes, rows):
        m = col.m[: 2 * feats, lanes]
        f1, f2 = m[:feats], m[feats:]
        cross = mm(win.key[rows, :], jnp.concatenate([f1, f1, f2, f2], 0))
        return cross, mm(win.vec[rows, :], col.vec[:, lanes])

    def weighed(lanes, rows, dots):
        far = beside([win.norm[rows, :]] * (width // z.own))
        weigh = jnp.exp(dots[0] - far - col.norm[:1, lanes]) * dots[1]
        g1 = weigh.astype(BF)
        g2 = (weigh - g1.astype(F32)).astype(BF)
        both = jnp.concatenate([g1, g2], 0)
        mine = win.m[:, rows]
        part = mm_nt(both, col.m[:, lanes])
        win.sums[rows, :] += part[:step] + part[step:]
        return mm(beside([mine, mine]), both)

    def first(lanes):
        return products(lanes, pl.ds(0, step)) if single else None

    def second(lanes, dots):
        if single:
            return weighed(lanes, pl.ds(0, step), dots)

        def add(k, sums):
            rows = pl.ds(k * step, step)
            return sums + weighed(lanes, rows, products(lanes, rows))

        return lax.fori_loop(0, z.wide // step, add, jnp.zeros((z.rows, width), F32))

    return first, second


def total_of(z, m, sums):
    feats = z.feats
    m = m[: 2 * feats].astype(F32)
    return sums[:feats] + sums[feats : 2 * feats] - (m[:feats] + m[feats:]) * sums[2 * feats : 2 * feats + 1]


def backprop(z, s, out_k, pack_ref):
    def first(lanes, total):
        t1, t2 = split(total)
        t_stack = stack([t1, t2])
        g = mm(out_k, jnp.concatenate([t_stack, t_stack], 0))
        both = mm_nt(beside([t_stack, t_stack]), beside([s.h1[:, lanes], s.h2[:, lanes]]))
        pack_ref[: z.feats] += both[: z.feats] + both[z.feats :]
        return g

    def second(lanes, g):
        h = s.h1[:, lanes].astype(F32) + s.h2[:, lanes].astype(F32)
        g = g * (1.0 - h * h)
        x_stack = stack(split(s.x[:, lanes]))
        g1 = g.astype(BF)
        g2 = (g - g1.astype(F32)).astype(BF)
        both = mm_nt(beside([x_stack, x_stack]), beside([g1, g2]))
        pack_ref[z.feats :] += both[: z.ins] + both[z.ins :]

    return first, second


def window_total(z, s, rows):
    return total_of(z, s.m[:, rows], s.sums[rows, :].T)


def column_steps(z, step):
    return [pl.ds(k * step, step) for k in range(z.cols // step)]


def column_features(z, blocks_ref, col, win, w_stack, out_m):
    column_blocks(z, blocks_ref, col)
    into, middle, out = network(z, col, w_stack, out_m)
    first, second = tile(z, win, col, z.early_step)
    lanes = column_steps(z, z.early_step)

    def third(k, raw):
        col.norm[:, lanes[k]] = jnp.broadcast_to(out(lanes[k], raw), (8, z.early_step))
        return first(lanes[k])

    def fourth(k, dots):
        col.sums[:, lanes[k]] = second(lanes[k], dots)

    flow(len(lanes), lambda k, _: into(lanes[k]), lambda k, pre: middle(lanes[k], pre), third, fourth)


def near_kernel(z, windows_ref, columns_ref, w_stack_ref, out_m_ref, *refs):
    n = len(z.windows())
    win, col = Refs(z.windows(), refs[:n]), Refs(z.columns(), refs[n:])
    w_stack, out_m = w_stack_ref[...], out_m_ref[...]
    window_features(z, windows_ref, win, w_stack, out_m)
    column_features(z, columns_ref, col, win, w_stack, out_m)


def far_kernel(z, columns_ref, w_stack_ref, out_m_ref, *refs):
    n, c = len(z.windows()), len(z.columns())
    win, col = Refs(z.windows(), refs[:n]), Refs(z.columns(), refs[n : n + c])
    sums_ref = refs[n + c]
    sums_ref[...] = win.sums[...]
    win.sums = sums_ref
    column_features(z, columns_ref, col, win, w_stack_ref[...], out_m_ref[...])


def late_kernel(z, windows_ref, w_stack_ref, out_m_ref, out_k_ref, *refs):
    w, c = len(z.windows()), len(z.columns())
    near = Refs(z.windows(), refs[:w])
    cols = [Refs(z.columns(), refs[w : w + c]), Refs(z.columns(), refs[w + c : w + 2 * c])]
    near.sums, col_grad_ref, pack_ref = refs[w + 2 * c : w + 2 * c + 3]
    win = Refs(z.windows(), refs[w + 2 * c + 3 :])
    out_k = out_k_ref[...]
    pack_ref[...] = jnp.zeros(pack_ref.shape, F32)
    rows = [pl.ds(i * z.win_step, z.win_step) for i in range(z.wide // z.win_step)]

    def backward(work, totals):
        stages = [backprop(z, s, out_k, pack_ref) for s, _ in work]
        first = [lambda k=k: stages[k][0](work[k][1], totals[k]()) for k in range(len(work))]
        second = [lambda g, k=k: stages[k][1](work[k][1], g) for k in range(len(work))]
        return first, second

    first, second = backward([(near, r) for r in rows], [functools.partial(window_total, z, near, r) for r in rows])
    window_features(z, windows_ref, win, w_stack_ref[...], out_m_ref[...], list(zip(first, second)))
    work = [(col, lanes) for col in cols for lanes in column_steps(z, z.col_step)]
    totals = []

    def total(k, dots):
        col, lanes = work[k]
        sums = col.sums[:, lanes] + tile(z, win, col, z.col_step)[1](lanes, dots)
        totals.append(total_of(z, col.m[:, lanes], sums))

    flow(len(work), lambda k, _: tile(z, win, work[k][0], z.col_step)[0](work[k][1]), total)
    col_grad_ref[...] = totals[0][:, : z.own]
    totals = [lambda t=t: t for t in totals] + [functools.partial(window_total, z, win, r) for r in rows]
    first, second = backward(work + [(win, r) for r in rows], totals)
    flow(len(first), lambda k, _: first[k](), lambda k, g: second[k](g))


def finish_kernel(z, mine_ref, theirs_ref, own_ref, col_grad_ref, grad_in_ref, grad_bias_ref, grad_out_ref):
    col_grad_ref[...] = own_ref[...]
    both = mine_ref[...] + theirs_ref[...]
    grad_out_ref[...] = both[: z.feats]
    grad_in_ref[...] = both[z.feats : z.feats + z.depth]
    grad_bias_ref[...] = both[z.feats + z.depth : z.feats + z.depth + 1]


def whole(count):
    return [pl.BlockSpec(memory_space=VMEM)] * count


def shapes(spec):
    return [jax.ShapeDtypeStruct(*v) for v in spec.values()]


def call(kernel, name, outs, operands, scratch=(), limit=4, cost=1, place=VMEM):
    return pl.pallas_call(
        kernel,
        out_shape=tuple(outs),
        in_specs=[pl.BlockSpec(memory_space=place)] * len(operands),
        out_specs=tuple(whole(len(outs))),
        scratch_shapes=list(scratch),
        compiler_params=pltpu.CompilerParams(vmem_limit_bytes=limit << 20),
        cost_estimate=pl.CostEstimate(flops=cost * 10**8, bytes_accessed=10**6, transcendentals=0),
        name=name,
    )(*operands)


def body(n_row, n_col, protocols, w_in, b_in, w_out, solved, probes, window_blocks):
    depth, own = protocols.shape
    z = Sizes(depth, solved.shape[0], w_out.shape[0], w_out.shape[1], own, n_row)
    bits = bits_of(n_col)
    joined = bits[1]
    shared = [bit for bit in bits if bit != joined]
    limit = 12 if n_row <= 4 else 48
    f32 = functools.partial(jax.ShapeDtypeStruct, dtype=F32)

    theirs = swap(protocols, "col", n_col, 1), swap(solved, "col", n_col, 1)
    blk = f32((z.part, own))
    window, columns, apart = call(
        functools.partial(prepare_kernel, z),
        "prepare",
        (blk, blk, jax.ShapeDtypeStruct((8, own), jnp.int32)),
        [pltpu.with_memory_space_constraint(v, pltpu.HBM) for v in (window_blocks, protocols, solved, probes)],
        [pltpu.SMEM(window_blocks.shape, jnp.int32), pltpu.SemaphoreType.DMA((4,))],
        place=pltpu.HBM,
    )
    (window,) = call(functools.partial(pick_kernel, z), "pick", (blk,), (window, apart, *theirs))

    def nearer(bit, mine, theirs):
        return jnp.where((apart[:1] & bit) == 0, mine, theirs)

    window, w_in, b_in, w_out = lax.optimization_barrier((window, w_in, b_in, w_out))
    w_stack, out_m, out_k = call(
        functools.partial(weights_kernel, z),
        "weights",
        (
            jax.ShapeDtypeStruct((z.hid, 6 * z.ins), BF),
            jax.ShapeDtypeStruct((2 * z.feats, z.hid), BF),
            jax.ShapeDtypeStruct((z.hid, 4 * z.feats), BF),
        ),
        (w_in[None], b_in.reshape(1, -1), w_out.T),
    )
    got = swap(jnp.concatenate([window, columns]), "col", n_col, joined)
    window = nearer(joined, window, got[: z.part])
    columns = jnp.concatenate([columns, got[z.part :]])
    window, w_stack, out_m, out_k = lax.optimization_barrier((window, w_stack, out_m, out_k))
    for bit in reversed(bits_of(n_row)[1:]):
        columns = jnp.concatenate([columns, swap(columns, "row", n_row, bit)])
    far_columns = swap(columns, "row", n_row, 1)
    for bit in shared[1:]:
        window = nearer(bit, window, swap(window, "col", n_col, bit))
    for bit in reversed(bits_of(n_row)[1:]):
        window = jnp.concatenate([window, swap(window, "row", n_row, bit)])
    far_window = swap(window, "row", n_row, 1)

    near = call(
        functools.partial(near_kernel, z),
        "near",
        (*shapes(z.windows()), *shapes(z.columns())),
        (window, columns, w_stack, out_m),
        limit=limit,
        cost=10,
    )
    windows, near = near[: len(z.windows())], near[len(z.windows()) :]
    *far, sums = call(
        functools.partial(far_kernel, z),
        "far",
        (*shapes(z.columns()), jax.ShapeDtypeStruct(*z.windows()["sums"])),
        (far_columns, w_stack, out_m, *windows),
        limit=limit,
        cost=10,
    )
    col_grad, pack = call(
        functools.partial(late_kernel, z),
        "late",
        (f32((z.feats, own)), f32((z.feats + z.ins, z.hid))),
        (far_window, w_stack, out_m, out_k, *windows, *near, *far, sums),
        [VMEM(*v) for v in z.windows().values()],
        limit=limit,
        cost=20,
    )
    for bit in reversed(shared[1:]):
        pack = pack + swap(pack, "col", n_col, bit)
    col_grad, grad_in, grad_bias, grad_out = call(
        functools.partial(finish_kernel, z),
        "finish",
        (f32((z.feats, own)), f32((depth, z.hid)), f32((1, z.hid)), f32((z.feats, z.hid))),
        (pack, swap(pack, "col", n_col, shared[0]), col_grad),
    )
    return (col_grad, grad_in, grad_bias.reshape(-1), grad_out.T)


def solution(mesh):
    n_row, n_col = mesh.shape["row"], mesh.shape["col"]
    cut = P(None, ("row", "col"))

    def per_device(*args):
        return body(n_row, n_col, *args)

    return jax.shard_map(
        per_device,
        mesh=mesh,
        in_specs=(cut, P(), P(), P(), cut, cut, P()),
        out_specs=(cut, P(), P(), P()),
        check_vma=False,
    )
```

```python
import functools

import jax
import jax.numpy as jnp
from jax import lax
from jax.experimental import pallas as pl
from jax.experimental.pallas import tpu as pltpu
from jax.sharding import PartitionSpec as P

BF, F32 = jnp.bfloat16, jnp.float32
VMEM = pltpu.VMEM


def swap(value, axis, size, bit):
    return lax.ppermute(value, axis, [(i, i ^ bit) for i in range(size)])


def bits_of(size):
    return [1 << k for k in range(size.bit_length() - 1)]


def split(value, terms=2):
    parts = []
    for _ in range(terms):
        part = value.astype(BF).astype(F32)
        parts.append(part)
        value = value - part
    return parts


def stack(parts):
    return jnp.concatenate(parts, 0).astype(BF)


def mm(a, b):
    return lax.dot_general(a, b, (((1,), (0,)), ((), ())), preferred_element_type=F32)


def mm_nt(a, b):
    return lax.dot_general(a, b, (((1,), (1,)), ((), ())), preferred_element_type=F32)


def each(count, step):
    if count <= 4:
        for i in range(count):
            step(i)
    else:
        lax.fori_loop(0, count, lambda i, c: (step(i), c)[1], 0)


def flow(count, *stages):
    held = {}
    for t in range(count + len(stages) - 1):
        for depth, stage in enumerate(stages):
            k = t - depth
            if 0 <= k < count:
                held[k] = stage(k, held.get(k))


def up(value, to):
    return -(-value // to) * to


class Sizes:
    def __init__(self, depth, vecs, hid, feats, own, n_row):
        self.depth, self.vecs, self.hid, self.feats, self.own = depth, vecs, hid, feats, own
        self.ins = up(depth + 1, 8)
        self.part = self.ins + vecs
        self.wide = n_row // 2 * own
        self.cols = n_row * own
        self.rows = 2 * feats + 16
        self.win_step = min(256, self.wide)
        self.col_step = min(512, self.cols)
        self.early_step = min(256, self.cols)

    def windows(self):
        w = self.wide
        return dict(
            x=((self.ins, w), F32),
            h1=((self.hid, w), BF),
            h2=((self.hid, w), BF),
            m=((self.rows, w), BF),
            right=((w, self.rows), BF),
            vec=((4 * self.vecs, w), BF),
            norm=((8, w), F32),
            sums=((self.rows, w), F32),
        )

    def columns(self):
        c = self.cols
        return dict(
            x=((self.ins, c), F32),
            h1=((c, self.hid), BF),
            h2=((c, self.hid), BF),
            slope=((c, self.hid), F32),
            pair=((c, 2 * self.feats), BF),
            m=((self.rows, c), BF),
            vec=((c, 4 * self.vecs), BF),
            norm=((c, self.own), F32),
            sums=((c, self.rows), F32),
        )


WEIGHTS = ("into", "out", "back")


class Refs:
    def __init__(self, names, refs):
        self.__dict__.update(zip(names, refs, strict=True))


def prepare_kernel(z, blocks_hbm, in_hbm, vec_hbm, probes_hbm, window_ref, columns_ref, apart_ref, blocks, sems):
    depth, ins = z.depth, z.ins
    moves = (
        (blocks_hbm, blocks),
        (in_hbm, window_ref.at[:depth]),
        (vec_hbm, window_ref.at[ins:]),
        (probes_hbm, columns_ref.at[ins:]),
    )
    copies = [pltpu.make_async_copy(src, dst, sems.at[i]) for i, (src, dst) in enumerate(moves)]
    for copy in copies:
        copy.start()
    for copy in copies:
        copy.wait()
    ones = jnp.where(lax.broadcasted_iota(jnp.int32, (ins - depth, z.own), 0) == 0, 1.0, 0.0)
    window_ref[depth:ins] = ones
    columns_ref[:depth] = window_ref[:depth]
    columns_ref[depth:ins] = ones
    apart_ref[...] = jnp.full(apart_ref.shape, blocks[lax.axis_index("row")] ^ lax.axis_index("col"), jnp.int32)


def pick_kernel(z, own_ref, apart_ref, far_in, far_vec, window_ref):
    depth, ins = z.depth, z.ins

    def nearer(mine, theirs):
        return jnp.where(jnp.broadcast_to(apart_ref[:1] & 1, mine.shape) == 0, mine, theirs)

    window_ref[:depth] = nearer(own_ref[:depth], far_in[...])
    window_ref[depth:ins] = own_ref[depth:ins]
    window_ref[ins:] = nearer(own_ref[ins:], far_vec[...])


def weights_kernel(z, w_in, b_in, w_out, *refs):
    col, win = Refs(WEIGHTS, refs[:3]), Refs(WEIGHTS, refs[3:])
    w_all = jnp.concatenate([w_in[0], b_in[...], jnp.zeros((z.ins - z.depth - 1, z.hid), F32)], 0)
    w1, w2, w3 = split(w_all, 3)
    w_stack = stack([w1, w1, w2, w2, w1, w3])
    col.into[...] = w_stack
    win.into[...] = w_stack.T
    o1, o2 = split(w_out[...])
    out = stack([o1, o2])
    win.out[...] = out
    col.out[...] = jnp.concatenate([out.T, out.T], 0)
    back = stack([o1, o1, o2, o2])
    col.back[...] = back
    win.back[...] = back.T


def beside(parts):
    return jnp.concatenate(parts, 1)


def both_halves(value):
    return value + pltpu.roll(value, value.shape[1] // 2, 1)


def paired(value):
    high = value.astype(BF).astype(F32)
    first = lax.broadcasted_iota(jnp.int32, value.shape, 1) < value.shape[1] // 2
    return jnp.where(first, high, value - high).astype(BF)


def column_network(z, s, w):
    def into(here):
        x1, x2, x3 = split(s.x[:, here], 3)
        return mm(stack([x1, x2, x1, x2, x3, x1]).T, w.into[...])

    def middle(here, pre):
        h = jnp.tanh(pre)
        h1 = h.astype(BF)
        h2 = (h - h1.astype(F32)).astype(BF)
        s.h1[here, :], s.h2[here, :] = h1, h2
        s.slope[here, :] = 1.0 - h * h
        return mm(beside([h1, h2]), w.out[...])

    def out(here, raw):
        pair = paired(both_halves(raw))
        s.pair[here, :] = pair
        s.m[: 2 * z.feats, here] = pair.T
        s.m[2 * z.feats :, here] = jnp.ones((16, raw.shape[0]), BF)
        return pair

    return into, middle, out


def window_network(z, s, w):
    def into(lanes):
        x1, x2, x3 = split(s.x[:, lanes], 3)
        return mm(w.into[...], stack([x1, x2, x1, x2, x3, x1]))

    def middle(lanes, pre):
        h = jnp.tanh(pre)
        h1 = h.astype(BF)
        h2 = (h - h1.astype(F32)).astype(BF)
        s.h1[:, lanes], s.h2[:, lanes] = h1, h2
        return mm(w.out[...], h1) + mm(w.out[...], h2)

    def out(lanes, raw):
        count = raw.shape[1]
        f1, f2 = split(raw[: z.feats] + raw[z.feats :])
        m = stack([f1, f2, jnp.ones((16, count), F32)])
        s.m[:, lanes] = m
        s.right[lanes, :] = m.T
        exact = f1 + f2
        s.norm[:, lanes] = jnp.broadcast_to(0.5 * jnp.sum(exact * exact, 0, keepdims=True), (8, count))

    return into, middle, out


def window_blocks(z, blocks_ref, s):
    own, part = z.own, z.part
    for r in range(z.wide // own):
        here = pl.ds(r * own, own)
        s.x[:, here] = blocks_ref[r * part : r * part + z.ins]
        v1, v2 = split(blocks_ref[r * part + z.ins : (r + 1) * part])
        s.vec[:, here] = stack([v1, v2, v1, v2])
    s.sums[...] = jnp.zeros(s.sums.shape, F32)


def column_blocks(z, blocks_ref, s):
    for r in range(z.cols // z.own):
        here = pl.ds(r * z.own, z.own)
        s.x[:, here] = blocks_ref[r * z.part : r * z.part + z.ins]
        v1, v2 = split(blocks_ref[r * z.part + z.ins : (r + 1) * z.part])
        s.vec[here, :] = stack([v1, v1, v2, v2]).T


def tile(z, win, col, width):
    feats, step = z.feats, z.win_step
    single = z.wide == step

    def products(lanes, rows):
        m = win.m[: 2 * feats, rows]
        f1, f2 = m[:feats], m[feats:]
        pair = col.pair[lanes, :]
        cross = mm(beside([pair, pair]), jnp.concatenate([f1, f1, f2, f2], 0))
        return cross, mm(col.vec[lanes, :], win.vec[:, rows])

    def weighed(lanes, rows, dots):
        own_norm = beside([col.norm[lanes, :]] * (step // z.own))
        weigh = jnp.exp(dots[0] - own_norm - win.norm[:1, rows]) * dots[1]
        g1 = weigh.astype(BF)
        g2 = (weigh - g1.astype(F32)).astype(BF)
        both = jnp.concatenate([g1, g2], 0)
        part = mm(both, win.right[rows, :])
        m = col.m[:, lanes]
        win.sums[:, rows] += mm(beside([m, m]), both)
        return part[:width] + part[width:]

    def first(lanes):
        return products(lanes, pl.ds(0, step)) if single else None

    def second(lanes, dots):
        if single:
            return weighed(lanes, pl.ds(0, step), dots)

        def add(k, sums):
            rows = pl.ds(k * step, step)
            return sums + weighed(lanes, rows, products(lanes, rows))

        return lax.fori_loop(0, z.wide // step, add, jnp.zeros((width, z.rows), F32))

    return first, second


def window_terms(z, s, rows):
    feats = z.feats
    m, sums = s.m[: 2 * feats, rows].astype(F32), s.sums[:, rows]
    total = sums[:feats] + sums[feats : 2 * feats] - (m[:feats] + m[feats:]) * sums[2 * feats : 2 * feats + 1]
    return stack(split(total))


def column_total(z, s, here, sums):
    wide = 2 * z.feats
    return both_halves(sums[:, :wide]) - both_halves(s.pair[here, :].astype(F32)) * sums[:, wide : wide + 1]


def column_terms(total):
    pair = paired(total)
    return pair.T, pair


def column_backprop(z, s, w, pack_ref):
    def first(here, terms):
        t_stack, pair = terms
        g = mm(beside([pair, pair]), w.back[...])
        both = mm(beside([t_stack, t_stack]), jnp.concatenate([s.h1[here, :], s.h2[here, :]], 0))
        pack_ref[: z.feats] += both[: z.feats] + both[z.feats :]
        return g

    def second(here, g):
        g = g * s.slope[here, :]
        x_stack = stack(split(s.x[:, here]))
        g1 = g.astype(BF)
        g2 = (g - g1.astype(F32)).astype(BF)
        both = mm(beside([x_stack, x_stack]), jnp.concatenate([g1, g2], 0))
        pack_ref[z.feats :] += both[: z.ins] + both[z.ins :]

    return first, second


def window_backprop(z, s, w, pack_ref):
    def first(lanes, t_stack):
        g = mm(w.back[...], jnp.concatenate([t_stack, t_stack], 0))
        both = mm_nt(beside([t_stack, t_stack]), beside([s.h1[:, lanes], s.h2[:, lanes]]))
        pack_ref[: z.feats] += both[: z.feats] + both[z.feats :]
        return g

    def second(lanes, g):
        h = s.h1[:, lanes].astype(F32) + s.h2[:, lanes].astype(F32)
        g = g * (1.0 - h * h)
        x_stack = stack(split(s.x[:, lanes]))
        g1 = g.astype(BF)
        g2 = (g - g1.astype(F32)).astype(BF)
        both = mm_nt(beside([x_stack, x_stack]), beside([g1, g2]))
        pack_ref[z.feats :] += both[: z.ins] + both[z.ins :]

    return first, second


def column_steps(z, step):
    return [pl.ds(k * step, step) for k in range(z.cols // step)]


def window_steps(z):
    return [pl.ds(k * z.win_step, z.win_step) for k in range(z.wide // z.win_step)]


def column_features(z, blocks_ref, col, win, w, w_win=None):
    column_blocks(z, blocks_ref, col)
    into, middle, out = column_network(z, col, w)
    first, second = tile(z, win, col, z.early_step)
    lanes = column_steps(z, z.early_step)
    rows = window_steps(z) if w_win else []
    stages = window_network(z, win, w_win) if w_win else ()

    def third(here, raw):
        out(here, raw)
        exact = both_halves(col.pair[here, :].astype(F32))
        norm = 0.25 * jnp.sum(exact * exact, 1, keepdims=True)
        col.norm[here, :] = jnp.broadcast_to(norm, (z.early_step, z.own))
        return first(here)

    def fourth(here, dots):
        col.sums[here, :] = second(here, dots)

    def stage(depth):
        def do(k, value):
            if k >= len(rows):
                here = lanes[k - len(rows)]
                return into(here) if depth == 0 else (middle, third, fourth)[depth - 1](here, value)
            if depth < 3:
                return stages[0](rows[k]) if depth == 0 else stages[depth](rows[k], value)

        return do

    flow(len(rows) + len(lanes), *[stage(depth) for depth in range(4)])


def near_kernel(z, windows_ref, columns_ref, *refs):
    n = len(z.windows())
    w_col, w_win, refs = Refs(WEIGHTS, refs[:3]), Refs(WEIGHTS, refs[3:6]), refs[6:]
    win, col = Refs(z.windows(), refs[:n]), Refs(z.columns(), refs[n:])
    window_blocks(z, windows_ref, win)
    column_features(z, columns_ref, col, win, w_col, w_win)


def far_kernel(z, columns_ref, *refs):
    n, c = len(z.windows()), len(z.columns())
    w_col, refs = Refs(WEIGHTS, refs[:3]), refs[3:]
    win, col = Refs(z.windows(), refs[:n]), Refs(z.columns(), refs[n : n + c])
    sums_ref = refs[n + c]
    sums_ref[...] = win.sums[...]
    win.sums = sums_ref
    column_features(z, columns_ref, col, win, w_col)


def late_kernel(z, windows_ref, *refs):
    n, c = len(z.windows()), len(z.columns())
    w_col, w_win, refs = Refs(WEIGHTS, refs[:3]), Refs(WEIGHTS, refs[3:6]), refs[6:]
    near = Refs(z.windows(), refs[:n])
    cols = [Refs(z.columns(), refs[n : n + c]), Refs(z.columns(), refs[n + c : n + 2 * c])]
    near.sums, col_grad_ref, pack_ref = refs[n + 2 * c : n + 2 * c + 3]
    win = Refs(z.windows(), refs[n + 2 * c + 3 :])
    pack_ref[...] = jnp.zeros(pack_ref.shape, F32)
    rows = window_steps(z)

    def of_window(s, here):
        first, second = window_backprop(z, s, w_win, pack_ref)
        return lambda: first(here, window_terms(z, s, here)), lambda g: second(here, g)

    def of_columns(s, here, total):
        first, second = column_backprop(z, s, w_col, pack_ref)
        return lambda: first(here, column_terms(total)), lambda g: second(here, g)

    window_blocks(z, windows_ref, win)
    into, middle, out = window_network(z, win, w_win)
    for here in rows:
        first, second = of_window(near, here)
        value = into(here)
        other = first()
        value = middle(here, value)
        second(other)
        out(here, value)
    work = [(col, lanes) for col in cols for lanes in column_steps(z, z.col_step)]
    totals = []

    def total(k, dots):
        col, lanes = work[k]
        sums = col.sums[lanes, :] + tile(z, win, col, z.col_step)[1](lanes, dots)
        totals.append(column_total(z, col, lanes, sums))

    flow(len(work), lambda k, _: tile(z, win, work[k][0], z.col_step)[0](work[k][1]), total)
    col_grad_ref[...] = totals[0][: z.own].T[: z.feats]
    stages = [of_columns(*item, t) for item, t in zip(work, totals)] + [of_window(win, here) for here in rows]
    flow(len(stages), lambda k, _: stages[k][0](), lambda k, g: stages[k][1](g))


def finish_kernel(z, mine_ref, theirs_ref, own_ref, col_grad_ref, grad_in_ref, grad_bias_ref, grad_out_ref):
    col_grad_ref[...] = own_ref[...]
    both = mine_ref[...] + theirs_ref[...]
    grad_out_ref[...] = both[: z.feats]
    grad_in_ref[...] = both[z.feats : z.feats + z.depth]
    grad_bias_ref[...] = both[z.feats + z.depth : z.feats + z.depth + 1]


def whole(count):
    return [pl.BlockSpec(memory_space=VMEM)] * count


def shapes(spec):
    return [jax.ShapeDtypeStruct(*v) for v in spec.values()]


def call(kernel, name, outs, operands, scratch=(), limit=4, cost=1, place=VMEM):
    return pl.pallas_call(
        kernel,
        out_shape=tuple(outs),
        in_specs=[pl.BlockSpec(memory_space=place)] * len(operands),
        out_specs=tuple(whole(len(outs))),
        scratch_shapes=list(scratch),
        compiler_params=pltpu.CompilerParams(vmem_limit_bytes=limit << 20),
        cost_estimate=pl.CostEstimate(flops=cost * 10**8, bytes_accessed=10**6, transcendentals=0),
        name=name,
    )(*operands)


def body(n_row, n_col, protocols, w_in, b_in, w_out, solved, probes, window_blocks):
    depth, own = protocols.shape
    z = Sizes(depth, solved.shape[0], w_out.shape[0], w_out.shape[1], own, n_row)
    bits = bits_of(n_col)
    joined = bits[1]
    shared = [bit for bit in bits if bit != joined]
    limit = 12 if n_row <= 4 else 48
    f32 = functools.partial(jax.ShapeDtypeStruct, dtype=F32)

    theirs = swap(protocols, "col", n_col, 1), swap(solved, "col", n_col, 1)
    blk = f32((z.part, own))
    window, columns, apart = call(
        functools.partial(prepare_kernel, z),
        "prepare",
        (blk, blk, jax.ShapeDtypeStruct((8, own), jnp.int32)),
        [pltpu.with_memory_space_constraint(v, pltpu.HBM) for v in (window_blocks, protocols, solved, probes)],
        [pltpu.SMEM(window_blocks.shape, jnp.int32), pltpu.SemaphoreType.DMA((4,))],
        place=pltpu.HBM,
    )
    (window,) = call(functools.partial(pick_kernel, z), "pick", (blk,), (window, apart, *theirs))

    def nearer(bit, mine, theirs):
        return jnp.where((apart[:1] & bit) == 0, mine, theirs)

    window, w_in, b_in, w_out = lax.optimization_barrier((window, w_in, b_in, w_out))
    forms = ((6 * z.ins, z.hid), (2 * z.hid, 2 * z.feats), (4 * z.feats, z.hid))
    forms += ((z.hid, 6 * z.ins), (2 * z.feats, z.hid), (z.hid, 4 * z.feats))
    weights = call(
        functools.partial(weights_kernel, z),
        "weights",
        [jax.ShapeDtypeStruct(form, BF) for form in forms],
        (w_in[None], b_in.reshape(1, -1), w_out.T),
    )
    got = swap(jnp.concatenate([window, columns]), "col", n_col, joined)
    window = nearer(joined, window, got[: z.part])
    columns = jnp.concatenate([columns, got[z.part :]])
    window, *weights = lax.optimization_barrier((window, *weights))
    for bit in reversed(bits_of(n_row)[1:]):
        columns = jnp.concatenate([columns, swap(columns, "row", n_row, bit)])
    far_columns = swap(columns, "row", n_row, 1)
    for bit in shared[1:]:
        window = nearer(bit, window, swap(window, "col", n_col, bit))
    for bit in reversed(bits_of(n_row)[1:]):
        window = jnp.concatenate([window, swap(window, "row", n_row, bit)])
    far_window = swap(window, "row", n_row, 1)

    near = call(
        functools.partial(near_kernel, z),
        "near",
        (*shapes(z.windows()), *shapes(z.columns())),
        (window, columns, *weights),
        limit=limit,
        cost=10,
    )
    windows, near = near[: len(z.windows())], near[len(z.windows()) :]
    *far, sums = call(
        functools.partial(far_kernel, z),
        "far",
        (*shapes(z.columns()), jax.ShapeDtypeStruct(*z.windows()["sums"])),
        (far_columns, *weights[:3], *windows),
        limit=limit,
        cost=10,
    )
    col_grad, pack = call(
        functools.partial(late_kernel, z),
        "late",
        (f32((z.feats, own)), f32((z.feats + z.ins, z.hid))),
        (far_window, *weights, *windows, *near, *far, sums),
        [VMEM(*v) for v in z.windows().values()],
        limit=limit,
        cost=20,
    )
    for bit in reversed(shared[1:]):
        pack = pack + swap(pack, "col", n_col, bit)
    col_grad, grad_in, grad_bias, grad_out = call(
        functools.partial(finish_kernel, z),
        "finish",
        (f32((z.feats, own)), f32((depth, z.hid)), f32((1, z.hid)), f32((z.feats, z.hid))),
        (pack, swap(pack, "col", n_col, shared[0]), col_grad),
    )
    return (col_grad, grad_in, grad_bias.reshape(-1), grad_out.T)


def solution(mesh):
    n_row, n_col = mesh.shape["row"], mesh.shape["col"]
    cut = P(None, ("row", "col"))

    def per_device(*args):
        return body(n_row, n_col, *args)

    return jax.shard_map(
        per_device,
        mesh=mesh,
        in_specs=(cut, P(), P(), P(), cut, cut, P()),
        out_specs=(cut, P(), P(), P()),
        check_vma=False,
    )
```

```python
import functools

import jax
import jax.numpy as jnp
from jax import lax
from jax.experimental import pallas as pl
from jax.experimental.pallas import tpu as pltpu
from jax.sharding import PartitionSpec as P

BF, F32 = jnp.bfloat16, jnp.float32
VMEM = pltpu.VMEM


def swap(value, axis, size, bit):
    return lax.ppermute(value, axis, [(i, i ^ bit) for i in range(size)])


def bits_of(size):
    return [1 << k for k in range(size.bit_length() - 1)]


def split(value, terms=2):
    parts = []
    for _ in range(terms):
        part = value.astype(BF).astype(F32)
        parts.append(part)
        value = value - part
    return parts


def stack(parts):
    return jnp.concatenate(parts, 0).astype(BF)


def mm(a, b):
    return lax.dot_general(a, b, (((1,), (0,)), ((), ())), preferred_element_type=F32)


def mm_nt(a, b):
    return lax.dot_general(a, b, (((1,), (1,)), ((), ())), preferred_element_type=F32)


def each(count, step):
    if count <= 4:
        for i in range(count):
            step(i)
    else:
        lax.fori_loop(0, count, lambda i, c: (step(i), c)[1], 0)


def flow(count, *stages):
    held = {}
    for t in range(count + len(stages) - 1):
        for depth, stage in enumerate(stages):
            k = t - depth
            if 0 <= k < count:
                held[k] = stage(k, held.get(k))


def up(value, to):
    return -(-value // to) * to


class Sizes:
    def __init__(self, depth, vecs, hid, feats, own, n_row):
        self.depth, self.vecs, self.hid, self.feats, self.own = depth, vecs, hid, feats, own
        self.ins = up(depth + 1, 8)
        self.part = self.ins + vecs
        self.wide = n_row // 2 * own
        self.cols = n_row * own
        self.rows = 2 * feats + 16
        self.win_step = min(256, self.wide)
        self.col_step = min(512, self.cols)
        self.early_step = min(256, self.cols)

    def windows(self):
        w = self.wide
        return dict(
            x=((self.ins, w), F32),
            h1=((self.hid, w), BF),
            h2=((self.hid, w), BF),
            m=((self.rows, w), BF),
            right=((w, self.rows), BF),
            vec=((4 * self.vecs, w), BF),
            norm=((8, w), F32),
            sums=((self.rows, w), F32),
        )

    def columns(self):
        c = self.cols
        return dict(
            x=((self.ins, c), F32),
            h1=((c, self.hid), BF),
            h2=((c, self.hid), BF),
            slope=((c, self.hid), F32),
            pair=((c, 2 * self.feats), BF),
            m=((self.rows, c), BF),
            vec=((c, 4 * self.vecs), BF),
            norm=((c, self.own), F32),
            sums=((c, self.rows), F32),
        )


WEIGHTS = ("into", "out", "back")


class Refs:
    def __init__(self, names, refs):
        self.__dict__.update(zip(names, refs, strict=True))


def prepare_kernel(z, blocks_hbm, in_hbm, vec_hbm, probes_hbm, window_ref, columns_ref, apart_ref, blocks, sems):
    depth, ins = z.depth, z.ins
    moves = (
        (blocks_hbm, blocks),
        (in_hbm, window_ref.at[:depth]),
        (vec_hbm, window_ref.at[ins:]),
        (probes_hbm, columns_ref.at[ins:]),
    )
    copies = [pltpu.make_async_copy(src, dst, sems.at[i]) for i, (src, dst) in enumerate(moves)]
    for copy in copies:
        copy.start()
    for copy in copies:
        copy.wait()
    ones = jnp.where(lax.broadcasted_iota(jnp.int32, (ins - depth, z.own), 0) == 0, 1.0, 0.0)
    window_ref[depth:ins] = ones
    columns_ref[:depth] = window_ref[:depth]
    columns_ref[depth:ins] = ones
    apart_ref[...] = jnp.full(apart_ref.shape, blocks[lax.axis_index("row")] ^ lax.axis_index("col"), jnp.int32)


def pick_kernel(z, own_ref, apart_ref, far_in, far_vec, window_ref):
    depth, ins = z.depth, z.ins

    def nearer(mine, theirs):
        return jnp.where(jnp.broadcast_to(apart_ref[:1] & 1, mine.shape) == 0, mine, theirs)

    window_ref[:depth] = nearer(own_ref[:depth], far_in[...])
    window_ref[depth:ins] = own_ref[depth:ins]
    window_ref[ins:] = nearer(own_ref[ins:], far_vec[...])


def weights_kernel(z, w_in, b_in, w_out, *refs):
    col, win = Refs(WEIGHTS, refs[:3]), Refs(WEIGHTS, refs[3:])
    w_all = jnp.concatenate([w_in[0], b_in[...], jnp.zeros((z.ins - z.depth - 1, z.hid), F32)], 0)
    w1, w2, w3 = split(w_all, 3)
    w_stack = stack([w1, w1, w2, w2, w1, w3])
    col.into[...] = w_stack
    win.into[...] = w_stack.T
    o1, o2 = split(w_out[...])
    out = stack([o1, o2])
    win.out[...] = out
    col.out[...] = jnp.concatenate([out.T, out.T], 0)
    back = stack([o1, o1, o2, o2])
    col.back[...] = back
    win.back[...] = back.T


def beside(parts):
    return jnp.concatenate(parts, 1)


def both_halves(value):
    return value + pltpu.roll(value, value.shape[1] // 2, 1)


def paired(value):
    high = value.astype(BF).astype(F32)
    first = lax.broadcasted_iota(jnp.int32, value.shape, 1) < value.shape[1] // 2
    return jnp.where(first, high, value - high).astype(BF)


def column_network(z, s, w):
    def into(here):
        x1, x2, x3 = split(s.x[:, here], 3)
        return mm(stack([x1, x2, x1, x2, x3, x1]).T, w.into[...])

    def middle(here, pre):
        h = jnp.tanh(pre)
        h1 = h.astype(BF)
        h2 = (h - h1.astype(F32)).astype(BF)
        s.h1[here, :], s.h2[here, :] = h1, h2
        s.slope[here, :] = 1.0 - h * h
        return mm(beside([h1, h2]), w.out[...])

    def out(here, raw):
        pair = paired(both_halves(raw))
        s.pair[here, :] = pair
        s.m[: 2 * z.feats, here] = pair.T
        s.m[2 * z.feats :, here] = jnp.ones((16, raw.shape[0]), BF)
        return pair

    return into, middle, out


def window_network(z, s, w):
    def into(lanes):
        x1, x2, x3 = split(s.x[:, lanes], 3)
        return mm(w.into[...], stack([x1, x2, x1, x2, x3, x1]))

    def middle(lanes, pre):
        h = jnp.tanh(pre)
        h1 = h.astype(BF)
        h2 = (h - h1.astype(F32)).astype(BF)
        s.h1[:, lanes], s.h2[:, lanes] = h1, h2
        return mm(w.out[...], h1) + mm(w.out[...], h2)

    def out(lanes, raw):
        count = raw.shape[1]
        f1, f2 = split(raw[: z.feats] + raw[z.feats :])
        m = stack([f1, f2, jnp.ones((16, count), F32)])
        s.m[:, lanes] = m
        s.right[lanes, :] = m.T
        exact = f1 + f2
        s.norm[:, lanes] = jnp.broadcast_to(0.5 * jnp.sum(exact * exact, 0, keepdims=True), (8, count))

    return into, middle, out


def window_blocks(z, blocks_ref, s):
    own, part = z.own, z.part
    for r in range(z.wide // own):
        here = pl.ds(r * own, own)
        s.x[:, here] = blocks_ref[r * part : r * part + z.ins]
        v1, v2 = split(blocks_ref[r * part + z.ins : (r + 1) * part])
        s.vec[:, here] = stack([v1, v2, v1, v2])
    s.sums[...] = jnp.zeros(s.sums.shape, F32)


def column_blocks(z, blocks_ref, s):
    for r in range(z.cols // z.own):
        here = pl.ds(r * z.own, z.own)
        s.x[:, here] = blocks_ref[r * z.part : r * z.part + z.ins]
        v1, v2 = split(blocks_ref[r * z.part + z.ins : (r + 1) * z.part])
        s.vec[here, :] = stack([v1, v1, v2, v2]).T


def tile(z, win, col, width):
    feats, step = z.feats, z.win_step
    single = z.wide == step

    def products(lanes, rows):
        m = win.m[: 2 * feats, rows]
        f1, f2 = m[:feats], m[feats:]
        pair = col.pair[lanes, :]
        cross = mm(beside([pair, pair]), jnp.concatenate([f1, f1, f2, f2], 0))
        return cross, mm(col.vec[lanes, :], win.vec[:, rows])

    def weighed(lanes, rows, dots):
        own_norm = beside([col.norm[lanes, :]] * (step // z.own))
        weigh = jnp.exp(dots[0] - own_norm - win.norm[:1, rows]) * dots[1]
        g1 = weigh.astype(BF)
        g2 = (weigh - g1.astype(F32)).astype(BF)
        both = jnp.concatenate([g1, g2], 0)
        part = mm(both, win.right[rows, :])
        m = col.m[:, lanes]
        win.sums[:, rows] += mm(beside([m, m]), both)
        return part[:width] + part[width:]

    def first(lanes):
        return products(lanes, pl.ds(0, step)) if single else None

    def second(lanes, dots):
        if single:
            return weighed(lanes, pl.ds(0, step), dots)

        def add(k, sums):
            rows = pl.ds(k * step, step)
            return sums + weighed(lanes, rows, products(lanes, rows))

        return lax.fori_loop(0, z.wide // step, add, jnp.zeros((width, z.rows), F32))

    return first, second


def window_terms(z, s, rows):
    feats = z.feats
    m, sums = s.m[: 2 * feats, rows].astype(F32), s.sums[:, rows]
    total = sums[:feats] + sums[feats : 2 * feats] - (m[:feats] + m[feats:]) * sums[2 * feats : 2 * feats + 1]
    return stack(split(total))


def column_total(z, s, here, sums):
    wide = 2 * z.feats
    return both_halves(sums[:, :wide]) - both_halves(s.pair[here, :].astype(F32)) * sums[:, wide : wide + 1]


def column_terms(total):
    pair = paired(total)
    return pair.T, pair


def column_backprop(z, s, w, pack_ref):
    def first(here, terms):
        t_stack, pair = terms
        g = mm(beside([pair, pair]), w.back[...])
        both = mm(beside([t_stack, t_stack]), jnp.concatenate([s.h1[here, :], s.h2[here, :]], 0))
        pack_ref[: z.feats] += both[: z.feats] + both[z.feats :]
        return g

    def second(here, g):
        g = g * s.slope[here, :]
        x_stack = stack(split(s.x[:, here]))
        g1 = g.astype(BF)
        g2 = (g - g1.astype(F32)).astype(BF)
        both = mm(beside([x_stack, x_stack]), jnp.concatenate([g1, g2], 0))
        pack_ref[z.feats :] += both[: z.ins] + both[z.ins :]

    return first, second


def window_backprop(z, s, w, pack_ref):
    def first(lanes, t_stack):
        g = mm(w.back[...], jnp.concatenate([t_stack, t_stack], 0))
        both = mm_nt(beside([t_stack, t_stack]), beside([s.h1[:, lanes], s.h2[:, lanes]]))
        pack_ref[: z.feats] += both[: z.feats] + both[z.feats :]
        return g

    def second(lanes, g):
        h = s.h1[:, lanes].astype(F32) + s.h2[:, lanes].astype(F32)
        g = g * (1.0 - h * h)
        x_stack = stack(split(s.x[:, lanes]))
        g1 = g.astype(BF)
        g2 = (g - g1.astype(F32)).astype(BF)
        both = mm_nt(beside([x_stack, x_stack]), beside([g1, g2]))
        pack_ref[z.feats :] += both[: z.ins] + both[z.ins :]

    return first, second


def column_steps(z, step):
    return [pl.ds(k * step, step) for k in range(z.cols // step)]


def window_steps(z):
    return [pl.ds(k * z.win_step, z.win_step) for k in range(z.wide // z.win_step)]


def column_features(z, blocks_ref, col, win, w, w_win=None):
    column_blocks(z, blocks_ref, col)
    into, middle, out = column_network(z, col, w)
    first, second = tile(z, win, col, z.early_step)
    lanes = column_steps(z, z.early_step)
    rows = window_steps(z) if w_win else []
    stages = window_network(z, win, w_win) if w_win else ()

    def third(here, raw):
        out(here, raw)
        exact = both_halves(col.pair[here, :].astype(F32))
        norm = 0.25 * jnp.sum(exact * exact, 1, keepdims=True)
        col.norm[here, :] = jnp.broadcast_to(norm, (z.early_step, z.own))
        return first(here)

    def fourth(here, dots):
        col.sums[here, :] = second(here, dots)

    def stage(depth):
        def do(k, value):
            if k >= len(rows):
                here = lanes[k - len(rows)]
                return into(here) if depth == 0 else (middle, third, fourth)[depth - 1](here, value)
            if depth < 3:
                return stages[0](rows[k]) if depth == 0 else stages[depth](rows[k], value)

        return do

    flow(len(rows) + len(lanes), *[stage(depth) for depth in range(4)])


def near_kernel(z, windows_ref, columns_ref, *refs):
    n = len(z.windows())
    w_col, w_win, refs = Refs(WEIGHTS, refs[:3]), Refs(WEIGHTS, refs[3:6]), refs[6:]
    win, col = Refs(z.windows(), refs[:n]), Refs(z.columns(), refs[n:])
    window_blocks(z, windows_ref, win)
    column_features(z, columns_ref, col, win, w_col, w_win)


def far_kernel(z, columns_ref, *refs):
    n, c = len(z.windows()), len(z.columns())
    w_col, refs = Refs(WEIGHTS, refs[:3]), refs[3:]
    win, col = Refs(z.windows(), refs[:n]), Refs(z.columns(), refs[n : n + c])
    sums_ref = refs[n + c]
    sums_ref[...] = win.sums[...]
    win.sums = sums_ref
    column_features(z, columns_ref, col, win, w_col)


def late_kernel(z, windows_ref, *refs):
    n, c = len(z.windows()), len(z.columns())
    w_col, w_win, refs = Refs(WEIGHTS, refs[:3]), Refs(WEIGHTS, refs[3:6]), refs[6:]
    near = Refs(z.windows(), refs[:n])
    cols = [Refs(z.columns(), refs[n : n + c]), Refs(z.columns(), refs[n + c : n + 2 * c])]
    near.sums, col_grad_ref, pack_ref = refs[n + 2 * c : n + 2 * c + 3]
    win = Refs(z.windows(), refs[n + 2 * c + 3 :])
    pack_ref[...] = jnp.zeros(pack_ref.shape, F32)
    rows = window_steps(z)

    def of_window(s, here):
        first, second = window_backprop(z, s, w_win, pack_ref)
        return lambda: first(here, window_terms(z, s, here)), lambda g: second(here, g)

    def of_columns(s, here, total):
        first, second = column_backprop(z, s, w_col, pack_ref)
        return lambda: first(here, column_terms(total)), lambda g: second(here, g)

    window_blocks(z, windows_ref, win)
    into, middle, out = window_network(z, win, w_win)
    for here in rows:
        first, second = of_window(near, here)
        value = into(here)
        other = first()
        value = middle(here, value)
        second(other)
        out(here, value)
    work = [(col, lanes) for col in cols for lanes in column_steps(z, z.col_step)]
    totals = []

    def total(k, dots):
        col, lanes = work[k]
        sums = col.sums[lanes, :] + tile(z, win, col, z.col_step)[1](lanes, dots)
        totals.append(column_total(z, col, lanes, sums))

    flow(len(work), lambda k, _: tile(z, win, work[k][0], z.col_step)[0](work[k][1]), total)
    col_grad_ref[...] = totals[0][: z.own].T[: z.feats]
    stages = [of_columns(*item, t) for item, t in zip(work, totals)] + [of_window(win, here) for here in rows]
    flow(len(stages), lambda k, _: stages[k][0](), lambda k, g: stages[k][1](g))


def emit_kernel(own_ref, col_grad_ref):
    col_grad_ref[...] = own_ref[...]


def finish_kernel(z, mine_ref, theirs_ref, grad_in_ref, grad_bias_ref, grad_out_ref):
    both = mine_ref[...] + theirs_ref[...]
    grad_out_ref[...] = both[: z.feats]
    grad_in_ref[...] = both[z.feats : z.feats + z.depth]
    grad_bias_ref[...] = both[z.feats + z.depth : z.feats + z.depth + 1]


def whole(count):
    return [pl.BlockSpec(memory_space=VMEM)] * count


def shapes(spec):
    return [jax.ShapeDtypeStruct(*v) for v in spec.values()]


def call(kernel, name, outs, operands, scratch=(), limit=4, cost=1, place=VMEM):
    return pl.pallas_call(
        kernel,
        out_shape=tuple(outs),
        in_specs=[pl.BlockSpec(memory_space=place)] * len(operands),
        out_specs=tuple(whole(len(outs))),
        scratch_shapes=list(scratch),
        compiler_params=pltpu.CompilerParams(vmem_limit_bytes=limit << 20),
        cost_estimate=pl.CostEstimate(flops=cost * 10**8, bytes_accessed=10**6, transcendentals=0),
        name=name,
    )(*operands)


def body(n_row, n_col, protocols, w_in, b_in, w_out, solved, probes, window_blocks):
    depth, own = protocols.shape
    z = Sizes(depth, solved.shape[0], w_out.shape[0], w_out.shape[1], own, n_row)
    bits = bits_of(n_col)
    joined = bits[1]
    shared = [bit for bit in bits if bit != joined]
    limit = 12 if n_row <= 4 else 48
    f32 = functools.partial(jax.ShapeDtypeStruct, dtype=F32)

    theirs = swap(protocols, "col", n_col, 1), swap(solved, "col", n_col, 1)
    blk = f32((z.part, own))
    window, columns, apart = call(
        functools.partial(prepare_kernel, z),
        "prepare",
        (blk, blk, jax.ShapeDtypeStruct((8, own), jnp.int32)),
        [pltpu.with_memory_space_constraint(v, pltpu.HBM) for v in (window_blocks, protocols, solved, probes)],
        [pltpu.SMEM(window_blocks.shape, jnp.int32), pltpu.SemaphoreType.DMA((4,))],
        place=pltpu.HBM,
    )
    (window,) = call(functools.partial(pick_kernel, z), "pick", (blk,), (window, apart, *theirs))

    def nearer(bit, mine, theirs):
        return jnp.where((apart[:1] & bit) == 0, mine, theirs)

    window, w_in, b_in, w_out = lax.optimization_barrier((window, w_in, b_in, w_out))
    forms = ((6 * z.ins, z.hid), (2 * z.hid, 2 * z.feats), (4 * z.feats, z.hid))
    forms += ((z.hid, 6 * z.ins), (2 * z.feats, z.hid), (z.hid, 4 * z.feats))
    weights = call(
        functools.partial(weights_kernel, z),
        "weights",
        [jax.ShapeDtypeStruct(form, BF) for form in forms],
        (w_in[None], b_in.reshape(1, -1), w_out.T),
    )
    got = swap(jnp.concatenate([window, columns]), "col", n_col, joined)
    window = nearer(joined, window, got[: z.part])
    columns = jnp.concatenate([columns, got[z.part :]])
    window, *weights = lax.optimization_barrier((window, *weights))
    for bit in reversed(bits_of(n_row)[1:]):
        columns = jnp.concatenate([columns, swap(columns, "row", n_row, bit)])
    far_columns = swap(columns, "row", n_row, 1)
    for bit in shared[1:]:
        window = nearer(bit, window, swap(window, "col", n_col, bit))
    for bit in reversed(bits_of(n_row)[1:]):
        window = jnp.concatenate([window, swap(window, "row", n_row, bit)])
    far_window = swap(window, "row", n_row, 1)

    near = call(
        functools.partial(near_kernel, z),
        "near",
        (*shapes(z.windows()), *shapes(z.columns())),
        (window, columns, *weights),
        limit=limit,
        cost=10,
    )
    windows, near = near[: len(z.windows())], near[len(z.windows()) :]
    *far, sums = call(
        functools.partial(far_kernel, z),
        "far",
        (*shapes(z.columns()), jax.ShapeDtypeStruct(*z.windows()["sums"])),
        (far_columns, *weights[:3], *windows),
        limit=limit,
        cost=10,
    )
    col_grad, pack = call(
        functools.partial(late_kernel, z),
        "late",
        (f32((z.feats, own)), f32((z.feats + z.ins, z.hid))),
        (far_window, *weights, *windows, *near, *far, sums),
        [VMEM(*v) for v in z.windows().values()],
        limit=limit,
        cost=20,
    )
    for bit in reversed(shared[1:]):
        pack = pack + swap(pack, "col", n_col, bit)
    (col_grad,) = call(emit_kernel, "emit", (f32((z.feats, own)),), (col_grad,))
    grad_in, grad_bias, grad_out = call(
        functools.partial(finish_kernel, z),
        "finish",
        (f32((depth, z.hid)), f32((1, z.hid)), f32((z.feats, z.hid))),
        (pack, swap(pack, "col", n_col, shared[0])),
    )
    return (col_grad, grad_in, grad_bias.reshape(-1), grad_out.T)


def solution(mesh):
    n_row, n_col = mesh.shape["row"], mesh.shape["col"]
    cut = P(None, ("row", "col"))

    def per_device(*args):
        return body(n_row, n_col, *args)

    return jax.shard_map(
        per_device,
        mesh=mesh,
        in_specs=(cut, P(), P(), P(), cut, cut, P()),
        out_specs=(cut, P(), P(), P()),
        check_vma=False,
    )
```

```python
import functools

import jax
import jax.numpy as jnp
from jax import lax
from jax.experimental import pallas as pl
from jax.experimental.pallas import tpu as pltpu
from jax.sharding import PartitionSpec as P

BF, F32 = jnp.bfloat16, jnp.float32
VMEM = pltpu.VMEM


def swap(value, axis, size, bit):
    return lax.ppermute(value, axis, [(i, i ^ bit) for i in range(size)])


def bits_of(size):
    return [1 << k for k in range(size.bit_length() - 1)]


def split(value, terms=2):
    parts = []
    for _ in range(terms):
        part = value.astype(BF).astype(F32)
        parts.append(part)
        value = value - part
    return parts


def stack(parts):
    return jnp.concatenate(parts, 0).astype(BF)


def mm(a, b):
    return lax.dot_general(a, b, (((1,), (0,)), ((), ())), preferred_element_type=F32)


def mm_nt(a, b):
    return lax.dot_general(a, b, (((1,), (1,)), ((), ())), preferred_element_type=F32)


def each(count, step):
    if count <= 4:
        for i in range(count):
            step(i)
    else:
        lax.fori_loop(0, count, lambda i, c: (step(i), c)[1], 0)


def flow(count, *stages):
    held = {}
    for t in range(count + len(stages) - 1):
        for depth, stage in enumerate(stages):
            k = t - depth
            if 0 <= k < count:
                held[k] = stage(k, held.get(k))


def up(value, to):
    return -(-value // to) * to


class Sizes:
    def __init__(self, depth, vecs, hid, feats, own, n_row):
        self.depth, self.vecs, self.hid, self.feats, self.own = depth, vecs, hid, feats, own
        self.ins = up(depth + 1, 8)
        self.part = self.ins + vecs
        self.wide = n_row // 2 * own
        self.cols = n_row * own
        self.rows = 2 * feats + 16
        self.win_step = min(256, self.wide)
        self.col_step = min(512, self.cols)
        self.early_step = min(256, self.cols)

    def windows(self):
        w = self.wide
        return dict(
            x=((self.ins, w), F32),
            h1=((self.hid, w), BF),
            h2=((self.hid, w), BF),
            m=((self.rows, w), BF),
            right=((w, self.rows), BF),
            vec=((4 * self.vecs, w), BF),
            norm=((8, w), F32),
            sums=((self.rows, w), F32),
        )

    def columns(self):
        c = self.cols
        return dict(
            x=((self.ins, c), F32),
            h1=((c, self.hid), BF),
            h2=((c, self.hid), BF),
            slope=((c, self.hid), F32),
            pair=((c, 2 * self.feats), BF),
            m=((self.rows, c), BF),
            vec=((c, 4 * self.vecs), BF),
            norm=((c, self.own), F32),
            sums=((c, self.rows), F32),
        )


WEIGHTS = ("into", "out", "back")


class Refs:
    def __init__(self, names, refs):
        self.__dict__.update(zip(names, refs, strict=True))


def prepare_kernel(z, blocks_hbm, in_hbm, vec_hbm, probes_hbm, window_ref, columns_ref, apart_ref, blocks, sems):
    depth, ins = z.depth, z.ins
    moves = (
        (blocks_hbm, blocks),
        (in_hbm, window_ref.at[:depth]),
        (vec_hbm, window_ref.at[ins:]),
        (probes_hbm, columns_ref.at[ins:]),
    )
    copies = [pltpu.make_async_copy(src, dst, sems.at[i]) for i, (src, dst) in enumerate(moves)]
    for copy in copies:
        copy.start()
    for copy in copies:
        copy.wait()
    ones = jnp.where(lax.broadcasted_iota(jnp.int32, (ins - depth, z.own), 0) == 0, 1.0, 0.0)
    window_ref[depth:ins] = ones
    columns_ref[:depth] = window_ref[:depth]
    columns_ref[depth:ins] = ones
    apart_ref[...] = jnp.full(apart_ref.shape, blocks[lax.axis_index("row")] ^ lax.axis_index("col"), jnp.int32)


def pick_kernel(z, own_ref, apart_ref, far_in, far_vec, window_ref):
    depth, ins = z.depth, z.ins

    def nearer(mine, theirs):
        return jnp.where(jnp.broadcast_to(apart_ref[:1] & 1, mine.shape) == 0, mine, theirs)

    window_ref[:depth] = nearer(own_ref[:depth], far_in[...])
    window_ref[depth:ins] = own_ref[depth:ins]
    window_ref[ins:] = nearer(own_ref[ins:], far_vec[...])


def weights_kernel(z, w_in, b_in, w_out, *refs):
    col, win = Refs(WEIGHTS, refs[:3]), Refs(WEIGHTS, refs[3:])
    w_all = jnp.concatenate([w_in[0], b_in[...], jnp.zeros((z.ins - z.depth - 1, z.hid), F32)], 0)
    w1, w2, w3 = split(w_all, 3)
    w_stack = stack([w1, w1, w2, w2, w1, w3])
    col.into[...] = w_stack
    win.into[...] = w_stack.T
    o1, o2 = split(w_out[...])
    out = stack([o1, o2])
    win.out[...] = out
    col.out[...] = jnp.concatenate([out.T, out.T], 0)
    back = stack([o1, o1, o2, o2])
    col.back[...] = back
    win.back[...] = back.T


def beside(parts):
    return jnp.concatenate(parts, 1)


def both_halves(value):
    return value + pltpu.roll(value, value.shape[1] // 2, 1)


def paired(value):
    high = value.astype(BF).astype(F32)
    first = lax.broadcasted_iota(jnp.int32, value.shape, 1) < value.shape[1] // 2
    return jnp.where(first, high, value - high).astype(BF)


def column_network(z, s, w):
    def into(here):
        x1, x2, x3 = split(s.x[:, here], 3)
        return mm(stack([x1, x2, x1, x2, x3, x1]).T, w.into[...])

    def middle(here, pre):
        h = jnp.tanh(pre)
        h1 = h.astype(BF)
        h2 = (h - h1.astype(F32)).astype(BF)
        s.h1[here, :], s.h2[here, :] = h1, h2
        s.slope[here, :] = 1.0 - h * h
        return mm(beside([h1, h2]), w.out[...])

    def out(here, raw):
        pair = paired(both_halves(raw))
        s.pair[here, :] = pair
        s.m[: 2 * z.feats, here] = pair.T
        s.m[2 * z.feats :, here] = jnp.ones((16, raw.shape[0]), BF)
        return pair

    return into, middle, out


def window_network(z, s, w):
    def into(lanes):
        x1, x2, x3 = split(s.x[:, lanes], 3)
        return mm(w.into[...], stack([x1, x2, x1, x2, x3, x1]))

    def middle(lanes, pre):
        h = jnp.tanh(pre)
        h1 = h.astype(BF)
        h2 = (h - h1.astype(F32)).astype(BF)
        s.h1[:, lanes], s.h2[:, lanes] = h1, h2
        return mm(w.out[...], h1) + mm(w.out[...], h2)

    def out(lanes, raw):
        count = raw.shape[1]
        f1, f2 = split(raw[: z.feats] + raw[z.feats :])
        m = stack([f1, f2, jnp.ones((16, count), F32)])
        s.m[:, lanes] = m
        s.right[lanes, :] = m.T
        exact = f1 + f2
        s.norm[:, lanes] = jnp.broadcast_to(0.5 * jnp.sum(exact * exact, 0, keepdims=True), (8, count))

    return into, middle, out


def window_blocks(z, blocks_ref, s):
    own, part = z.own, z.part
    for r in range(z.wide // own):
        here = pl.ds(r * own, own)
        s.x[:, here] = blocks_ref[r * part : r * part + z.ins]
        v1, v2 = split(blocks_ref[r * part + z.ins : (r + 1) * part])
        s.vec[:, here] = stack([v1, v2, v1, v2])
    s.sums[...] = jnp.zeros(s.sums.shape, F32)


def column_blocks(z, blocks_ref, s):
    for r in range(z.cols // z.own):
        here = pl.ds(r * z.own, z.own)
        s.x[:, here] = blocks_ref[r * z.part : r * z.part + z.ins]
        v1, v2 = split(blocks_ref[r * z.part + z.ins : (r + 1) * z.part])
        s.vec[here, :] = stack([v1, v1, v2, v2]).T


def tile(z, win, col, width):
    feats, step = z.feats, z.win_step
    single = z.wide == step

    def products(lanes, rows):
        m = win.m[: 2 * feats, rows]
        f1, f2 = m[:feats], m[feats:]
        pair = col.pair[lanes, :]
        cross = mm(beside([pair, pair]), jnp.concatenate([f1, f1, f2, f2], 0))
        return cross, mm(col.vec[lanes, :], win.vec[:, rows])

    def weighed(lanes, rows, dots):
        own_norm = beside([col.norm[lanes, :]] * (step // z.own))
        weigh = jnp.exp(dots[0] - own_norm - win.norm[:1, rows]) * dots[1]
        g1 = weigh.astype(BF)
        g2 = (weigh - g1.astype(F32)).astype(BF)
        both = jnp.concatenate([g1, g2], 0)
        part = mm(both, win.right[rows, :])
        m = col.m[:, lanes]
        win.sums[:, rows] += mm(beside([m, m]), both)
        return part[:width] + part[width:]

    def first(lanes):
        return products(lanes, pl.ds(0, step)) if single else None

    def second(lanes, dots):
        if single:
            return weighed(lanes, pl.ds(0, step), dots)

        def add(k, sums):
            rows = pl.ds(k * step, step)
            return sums + weighed(lanes, rows, products(lanes, rows))

        return lax.fori_loop(0, z.wide // step, add, jnp.zeros((width, z.rows), F32))

    return first, second


def window_terms(z, s, rows):
    feats = z.feats
    m, sums = s.m[: 2 * feats, rows].astype(F32), s.sums[:, rows]
    total = sums[:feats] + sums[feats : 2 * feats] - (m[:feats] + m[feats:]) * sums[2 * feats : 2 * feats + 1]
    return stack(split(total))


def column_total(z, s, here, sums):
    wide = 2 * z.feats
    return both_halves(sums[:, :wide]) - both_halves(s.pair[here, :].astype(F32)) * sums[:, wide : wide + 1]


def column_terms(total):
    pair = paired(total)
    return pair.T, pair


def column_backprop(z, s, w, pack_ref):
    def first(here, terms):
        t_stack, pair = terms
        g = mm(beside([pair, pair]), w.back[...])
        both = mm(t_stack, s.h1[here, :])
        pack_ref[: z.feats] += both[: z.feats] + both[z.feats :] + mm(t_stack[: z.feats], s.h2[here, :])
        return g

    def second(here, g):
        g = g * s.slope[here, :]
        x_stack = stack(split(s.x[:, here]))
        g1 = g.astype(BF)
        g2 = (g - g1.astype(F32)).astype(BF)
        both = mm(beside([x_stack, x_stack]), jnp.concatenate([g1, g2], 0))
        pack_ref[z.feats :] += both[: z.ins] + both[z.ins :]

    return first, second


def window_backprop(z, s, w, pack_ref):
    def first(lanes, t_stack):
        g = mm(w.back[...], jnp.concatenate([t_stack, t_stack], 0))
        both = mm_nt(beside([t_stack, t_stack]), beside([s.h1[:, lanes], s.h2[:, lanes]]))
        pack_ref[: z.feats] += both[: z.feats] + both[z.feats :]
        return g

    def second(lanes, g):
        h = s.h1[:, lanes].astype(F32) + s.h2[:, lanes].astype(F32)
        g = g * (1.0 - h * h)
        x_stack = stack(split(s.x[:, lanes]))
        g1 = g.astype(BF)
        g2 = (g - g1.astype(F32)).astype(BF)
        both = mm_nt(beside([x_stack, x_stack]), beside([g1, g2]))
        pack_ref[z.feats :] += both[: z.ins] + both[z.ins :]

    return first, second


def column_steps(z, step):
    return [pl.ds(k * step, step) for k in range(z.cols // step)]


def window_steps(z):
    return [pl.ds(k * z.win_step, z.win_step) for k in range(z.wide // z.win_step)]


def column_features(z, blocks_ref, col, win, w, w_win=None):
    column_blocks(z, blocks_ref, col)
    into, middle, out = column_network(z, col, w)
    first, second = tile(z, win, col, z.early_step)
    lanes = column_steps(z, z.early_step)
    rows = window_steps(z) if w_win else []
    stages = window_network(z, win, w_win) if w_win else ()

    def third(here, raw):
        out(here, raw)
        exact = both_halves(col.pair[here, :].astype(F32))
        norm = 0.25 * jnp.sum(exact * exact, 1, keepdims=True)
        col.norm[here, :] = jnp.broadcast_to(norm, (z.early_step, z.own))
        return first(here)

    def fourth(here, dots):
        col.sums[here, :] = second(here, dots)

    def stage(depth):
        def do(k, value):
            if k >= len(rows):
                here = lanes[k - len(rows)]
                return into(here) if depth == 0 else (middle, third, fourth)[depth - 1](here, value)
            if depth < 3:
                return stages[0](rows[k]) if depth == 0 else stages[depth](rows[k], value)

        return do

    flow(len(rows) + len(lanes), *[stage(depth) for depth in range(4)])


def near_kernel(z, windows_ref, columns_ref, *refs):
    n = len(z.windows())
    w_col, w_win, refs = Refs(WEIGHTS, refs[:3]), Refs(WEIGHTS, refs[3:6]), refs[6:]
    win, col = Refs(z.windows(), refs[:n]), Refs(z.columns(), refs[n:])
    window_blocks(z, windows_ref, win)
    column_features(z, columns_ref, col, win, w_col, w_win)


def far_kernel(z, columns_ref, *refs):
    n, c = len(z.windows()), len(z.columns())
    w_col, refs = Refs(WEIGHTS, refs[:3]), refs[3:]
    win, col = Refs(z.windows(), refs[:n]), Refs(z.columns(), refs[n : n + c])
    sums_ref = refs[n + c]
    sums_ref[...] = win.sums[...]
    win.sums = sums_ref
    column_features(z, columns_ref, col, win, w_col)


def late_kernel(z, windows_ref, *refs):
    n, c = len(z.windows()), len(z.columns())
    w_col, w_win, refs = Refs(WEIGHTS, refs[:3]), Refs(WEIGHTS, refs[3:6]), refs[6:]
    near = Refs(z.windows(), refs[:n])
    cols = [Refs(z.columns(), refs[n : n + c]), Refs(z.columns(), refs[n + c : n + 2 * c])]
    near.sums, col_grad_ref, pack_ref = refs[n + 2 * c : n + 2 * c + 3]
    win = Refs(z.windows(), refs[n + 2 * c + 3 :])
    pack_ref[...] = jnp.zeros(pack_ref.shape, F32)
    rows = window_steps(z)

    def of_window(s, here):
        first, second = window_backprop(z, s, w_win, pack_ref)
        return lambda: first(here, window_terms(z, s, here)), lambda g: second(here, g)

    def of_columns(s, here, total):
        first, second = column_backprop(z, s, w_col, pack_ref)
        return lambda: first(here, column_terms(total)), lambda g: second(here, g)

    window_blocks(z, windows_ref, win)
    into, middle, out = window_network(z, win, w_win)
    for here in rows:
        first, second = of_window(near, here)
        value = into(here)
        other = first()
        value = middle(here, value)
        second(other)
        out(here, value)
    work = [(col, lanes) for col in cols for lanes in column_steps(z, z.col_step)]
    totals = []

    def total(k, dots):
        col, lanes = work[k]
        sums = col.sums[lanes, :] + tile(z, win, col, z.col_step)[1](lanes, dots)
        totals.append(column_total(z, col, lanes, sums))

    flow(len(work), lambda k, _: tile(z, win, work[k][0], z.col_step)[0](work[k][1]), total)
    col_grad_ref[...] = totals[0][: z.own].T[: z.feats]
    stages = [of_columns(*item, t) for item, t in zip(work, totals)] + [of_window(win, here) for here in rows]
    flow(len(stages), lambda k, _: stages[k][0](), lambda k, g: stages[k][1](g))


def emit_kernel(own_ref, col_grad_ref):
    col_grad_ref[...] = own_ref[...]


def finish_kernel(z, mine_ref, theirs_ref, grad_in_ref, grad_bias_ref, grad_out_ref):
    both = mine_ref[...] + theirs_ref[...]
    grad_out_ref[...] = both[: z.feats]
    grad_in_ref[...] = both[z.feats : z.feats + z.depth]
    grad_bias_ref[...] = both[z.feats + z.depth : z.feats + z.depth + 1]


def whole(count):
    return [pl.BlockSpec(memory_space=VMEM)] * count


def shapes(spec):
    return [jax.ShapeDtypeStruct(*v) for v in spec.values()]


def call(kernel, name, outs, operands, scratch=(), limit=4, cost=1, place=VMEM):
    return pl.pallas_call(
        kernel,
        out_shape=tuple(outs),
        in_specs=[pl.BlockSpec(memory_space=place)] * len(operands),
        out_specs=tuple(whole(len(outs))),
        scratch_shapes=list(scratch),
        compiler_params=pltpu.CompilerParams(vmem_limit_bytes=limit << 20),
        cost_estimate=pl.CostEstimate(flops=cost * 10**8, bytes_accessed=10**6, transcendentals=0),
        name=name,
    )(*operands)


def body(n_row, n_col, protocols, w_in, b_in, w_out, solved, probes, window_blocks):
    depth, own = protocols.shape
    z = Sizes(depth, solved.shape[0], w_out.shape[0], w_out.shape[1], own, n_row)
    bits = bits_of(n_col)
    joined = bits[1]
    shared = [bit for bit in bits if bit != joined]
    limit = 12 if n_row <= 4 else 48
    f32 = functools.partial(jax.ShapeDtypeStruct, dtype=F32)

    theirs = swap(protocols, "col", n_col, 1), swap(solved, "col", n_col, 1)
    blk = f32((z.part, own))
    window, columns, apart = call(
        functools.partial(prepare_kernel, z),
        "prepare",
        (blk, blk, jax.ShapeDtypeStruct((8, own), jnp.int32)),
        [pltpu.with_memory_space_constraint(v, pltpu.HBM) for v in (window_blocks, protocols, solved, probes)],
        [pltpu.SMEM(window_blocks.shape, jnp.int32), pltpu.SemaphoreType.DMA((4,))],
        place=pltpu.HBM,
    )
    (window,) = call(functools.partial(pick_kernel, z), "pick", (blk,), (window, apart, *theirs))

    def nearer(bit, mine, theirs):
        return jnp.where((apart[:1] & bit) == 0, mine, theirs)

    window, w_in, b_in, w_out = lax.optimization_barrier((window, w_in, b_in, w_out))
    forms = ((6 * z.ins, z.hid), (2 * z.hid, 2 * z.feats), (4 * z.feats, z.hid))
    forms += ((z.hid, 6 * z.ins), (2 * z.feats, z.hid), (z.hid, 4 * z.feats))
    weights = call(
        functools.partial(weights_kernel, z),
        "weights",
        [jax.ShapeDtypeStruct(form, BF) for form in forms],
        (w_in[None], b_in.reshape(1, -1), w_out.T),
    )
    got = swap(jnp.concatenate([window, columns]), "col", n_col, joined)
    window = nearer(joined, window, got[: z.part])
    columns = jnp.concatenate([columns, got[z.part :]])
    window, *weights = lax.optimization_barrier((window, *weights))
    for bit in reversed(bits_of(n_row)[1:]):
        columns = jnp.concatenate([columns, swap(columns, "row", n_row, bit)])
    far_columns = swap(columns, "row", n_row, 1)
    for bit in shared[1:]:
        window = nearer(bit, window, swap(window, "col", n_col, bit))
    for bit in reversed(bits_of(n_row)[1:]):
        window = jnp.concatenate([window, swap(window, "row", n_row, bit)])
    far_window = swap(window, "row", n_row, 1)

    near = call(
        functools.partial(near_kernel, z),
        "near",
        (*shapes(z.windows()), *shapes(z.columns())),
        (window, columns, *weights),
        limit=limit,
        cost=10,
    )
    windows, near = near[: len(z.windows())], near[len(z.windows()) :]
    *far, sums = call(
        functools.partial(far_kernel, z),
        "far",
        (*shapes(z.columns()), jax.ShapeDtypeStruct(*z.windows()["sums"])),
        (far_columns, *weights[:3], *windows),
        limit=limit,
        cost=10,
    )
    col_grad, pack = call(
        functools.partial(late_kernel, z),
        "late",
        (f32((z.feats, own)), f32((z.feats + z.ins, z.hid))),
        (far_window, *weights, *windows, *near, *far, sums),
        [VMEM(*v) for v in z.windows().values()],
        limit=limit,
        cost=20,
    )
    for bit in reversed(shared[1:]):
        pack = pack + swap(pack, "col", n_col, bit)
    (col_grad,) = call(emit_kernel, "emit", (f32((z.feats, own)),), (col_grad,))
    grad_in, grad_bias, grad_out = call(
        functools.partial(finish_kernel, z),
        "finish",
        (f32((depth, z.hid)), f32((1, z.hid)), f32((z.feats, z.hid))),
        (pack, swap(pack, "col", n_col, shared[0])),
    )
    return (col_grad, grad_in, grad_bias.reshape(-1), grad_out.T)


def solution(mesh):
    n_row, n_col = mesh.shape["row"], mesh.shape["col"]
    cut = P(None, ("row", "col"))

    def per_device(*args):
        return body(n_row, n_col, *args)

    return jax.shard_map(
        per_device,
        mesh=mesh,
        in_specs=(cut, P(), P(), P(), cut, cut, P()),
        out_specs=(cut, P(), P(), P()),
        check_vma=False,
    )
```

```python
import functools

import jax
import jax.numpy as jnp
from jax import lax
from jax.experimental import pallas as pl
from jax.experimental.pallas import tpu as pltpu
from jax.sharding import PartitionSpec as P

BF, F32 = jnp.bfloat16, jnp.float32
VMEM = pltpu.VMEM


def swap(value, axis, size, bit):
    return lax.ppermute(value, axis, [(i, i ^ bit) for i in range(size)])


def bits_of(size):
    return [1 << k for k in range(size.bit_length() - 1)]


def split(value, terms=2):
    parts = []
    for _ in range(terms):
        part = value.astype(BF).astype(F32)
        parts.append(part)
        value = value - part
    return parts


def stack(parts):
    return jnp.concatenate(parts, 0).astype(BF)


def mm(a, b):
    return lax.dot_general(a, b, (((1,), (0,)), ((), ())), preferred_element_type=F32)


def mm_nt(a, b):
    return lax.dot_general(a, b, (((1,), (1,)), ((), ())), preferred_element_type=F32)


def each(count, step):
    if count <= 4:
        for i in range(count):
            step(i)
    else:
        lax.fori_loop(0, count, lambda i, c: (step(i), c)[1], 0)


def flow(count, *stages):
    held = {}
    for t in range(count + len(stages) - 1):
        for depth, stage in enumerate(stages):
            k = t - depth
            if 0 <= k < count:
                held[k] = stage(k, held.get(k))


def up(value, to):
    return -(-value // to) * to


class Sizes:
    def __init__(self, depth, vecs, hid, feats, own, n_row):
        self.depth, self.vecs, self.hid, self.feats, self.own = depth, vecs, hid, feats, own
        self.ins = up(depth + 1, 8)
        self.part = self.ins + vecs
        self.wide = n_row // 2 * own
        self.cols = n_row * own
        self.rows = 2 * feats + 16
        self.win_step = min(256, self.wide)
        self.col_step = min(512, self.cols)
        self.early_step = min(256, self.cols)

    def windows(self):
        w = self.wide
        return dict(
            x=((self.ins, w), F32),
            h1=((self.hid, w), BF),
            h2=((self.hid, w), BF),
            m=((self.rows, w), BF),
            right=((w, self.rows), BF),
            vec=((4 * self.vecs, w), BF),
            norm=((8, w), F32),
            sums=((self.rows, w), F32),
        )

    def columns(self):
        c = self.cols
        return dict(
            x=((self.ins, c), F32),
            h1=((c, self.hid), BF),
            h2=((c, self.hid), BF),
            slope=((c, self.hid), F32),
            pair=((c, 2 * self.feats), BF),
            m=((self.rows, c), BF),
            vec=((c, 4 * self.vecs), BF),
            norm=((c, self.own), F32),
            sums=((c, self.rows), F32),
        )


WEIGHTS = ("into", "out", "back")


class Refs:
    def __init__(self, names, refs):
        self.__dict__.update(zip(names, refs, strict=True))


def prepare_kernel(z, blocks_hbm, in_hbm, vec_hbm, probes_hbm, window_ref, columns_ref, apart_ref, blocks, sems):
    depth, ins = z.depth, z.ins
    moves = (
        (blocks_hbm, blocks),
        (in_hbm, window_ref.at[:depth]),
        (vec_hbm, window_ref.at[ins:]),
        (probes_hbm, columns_ref.at[ins:]),
    )
    copies = [pltpu.make_async_copy(src, dst, sems.at[i]) for i, (src, dst) in enumerate(moves)]
    for copy in copies:
        copy.start()
    for copy in copies:
        copy.wait()
    ones = jnp.where(lax.broadcasted_iota(jnp.int32, (ins - depth, z.own), 0) == 0, 1.0, 0.0)
    window_ref[depth:ins] = ones
    columns_ref[:depth] = window_ref[:depth]
    columns_ref[depth:ins] = ones
    apart_ref[...] = jnp.full(apart_ref.shape, blocks[lax.axis_index("row")] ^ lax.axis_index("col"), jnp.int32)


def pick_kernel(z, own_ref, apart_ref, far_in, far_vec, window_ref):
    depth, ins = z.depth, z.ins

    def nearer(mine, theirs):
        return jnp.where(jnp.broadcast_to(apart_ref[:1] & 1, mine.shape) == 0, mine, theirs)

    window_ref[:depth] = nearer(own_ref[:depth], far_in[...])
    window_ref[depth:ins] = own_ref[depth:ins]
    window_ref[ins:] = nearer(own_ref[ins:], far_vec[...])


def weights_kernel(z, w_in, b_in, w_out, *refs):
    col, win = Refs(WEIGHTS, refs[:3]), Refs(WEIGHTS, refs[3:])
    w_all = jnp.concatenate([w_in[0], b_in[...], jnp.zeros((z.ins - z.depth - 1, z.hid), F32)], 0)
    w1, w2, w3 = split(w_all, 3)
    w_stack = stack([w1, w1, w2, w2, w1, w3])
    col.into[...] = w_stack
    win.into[...] = w_stack.T
    o1, o2 = split(w_out[...])
    out = stack([o1, o2])
    win.out[...] = out
    col.out[...] = jnp.concatenate([out.T, out.T], 0)
    back = stack([o1, o1, o2, o2])
    col.back[...] = back
    win.back[...] = back.T


def beside(parts):
    return jnp.concatenate(parts, 1)


def both_halves(value):
    return value + pltpu.roll(value, value.shape[1] // 2, 1)


def paired(value):
    high = value.astype(BF).astype(F32)
    first = lax.broadcasted_iota(jnp.int32, value.shape, 1) < value.shape[1] // 2
    return jnp.where(first, high, value - high).astype(BF)


def column_network(z, s, w):
    def into(here):
        x1, x2, x3 = split(s.x[:, here], 3)
        return mm(stack([x1, x2, x1, x2, x3, x1]).T, w.into[...])

    def middle(here, pre):
        h = jnp.tanh(pre)
        h1 = h.astype(BF)
        h2 = (h - h1.astype(F32)).astype(BF)
        s.h1[here, :], s.h2[here, :] = h1, h2
        s.slope[here, :] = 1.0 - h * h
        return mm(beside([h1, h2]), w.out[...])

    def out(here, raw):
        pair = paired(both_halves(raw))
        s.pair[here, :] = pair
        s.m[: 2 * z.feats, here] = pair.T
        s.m[2 * z.feats :, here] = jnp.ones((16, raw.shape[0]), BF)
        return pair

    return into, middle, out


def window_network(z, s, w):
    def into(lanes):
        x1, x2, x3 = split(s.x[:, lanes], 3)
        return mm(w.into[...], stack([x1, x2, x1, x2, x3, x1]))

    def middle(lanes, pre):
        h = jnp.tanh(pre)
        h1 = h.astype(BF)
        h2 = (h - h1.astype(F32)).astype(BF)
        s.h1[:, lanes], s.h2[:, lanes] = h1, h2
        return mm(w.out[...], h1) + mm(w.out[...], h2)

    def out(lanes, raw):
        count = raw.shape[1]
        f1, f2 = split(raw[: z.feats] + raw[z.feats :])
        m = stack([f1, f2, jnp.ones((16, count), F32)])
        s.m[:, lanes] = m
        s.right[lanes, :] = m.T
        exact = f1 + f2
        s.norm[:, lanes] = jnp.broadcast_to(0.5 * jnp.sum(exact * exact, 0, keepdims=True), (8, count))

    return into, middle, out


def window_blocks(z, blocks_ref, s):
    own, part = z.own, z.part
    for r in range(z.wide // own):
        here = pl.ds(r * own, own)
        s.x[:, here] = blocks_ref[r * part : r * part + z.ins]
        v1, v2 = split(blocks_ref[r * part + z.ins : (r + 1) * part])
        s.vec[:, here] = stack([v1, v2, v1, v2])
    s.sums[...] = jnp.zeros(s.sums.shape, F32)


def column_blocks(z, blocks_ref, s):
    for r in range(z.cols // z.own):
        here = pl.ds(r * z.own, z.own)
        s.x[:, here] = blocks_ref[r * z.part : r * z.part + z.ins]
        v1, v2 = split(blocks_ref[r * z.part + z.ins : (r + 1) * z.part])
        s.vec[here, :] = stack([v1, v1, v2, v2]).T


def tile(z, win, col, width):
    feats, step = z.feats, z.win_step
    single = z.wide == step

    def products(lanes, rows):
        m = win.m[: 2 * feats, rows]
        f1, f2 = m[:feats], m[feats:]
        pair = col.pair[lanes, :]
        cross = mm(beside([pair, pair]), jnp.concatenate([f1, f1, f2, f2], 0))
        return cross, mm(col.vec[lanes, :], win.vec[:, rows])

    def weighed(lanes, rows, dots):
        own_norm = beside([col.norm[lanes, :]] * (step // z.own))
        weigh = jnp.exp(dots[0] - own_norm - win.norm[:1, rows]) * dots[1]
        g1 = weigh.astype(BF)
        g2 = (weigh - g1.astype(F32)).astype(BF)
        both = jnp.concatenate([g1, g2], 0)
        part = mm(both, win.right[rows, :])
        m = col.m[:, lanes]
        win.sums[:, rows] += mm(beside([m, m]), both)
        return part[:width] + part[width:]

    def first(lanes):
        return products(lanes, pl.ds(0, step)) if single else None

    def second(lanes, dots):
        if single:
            return weighed(lanes, pl.ds(0, step), dots)

        def add(k, sums):
            rows = pl.ds(k * step, step)
            return sums + weighed(lanes, rows, products(lanes, rows))

        return lax.fori_loop(0, z.wide // step, add, jnp.zeros((width, z.rows), F32))

    return first, second


def window_terms(z, s, rows):
    feats = z.feats
    m, sums = s.m[: 2 * feats, rows].astype(F32), s.sums[:, rows]
    total = sums[:feats] + sums[feats : 2 * feats] - (m[:feats] + m[feats:]) * sums[2 * feats : 2 * feats + 1]
    return stack(split(total))


def column_total(z, s, here, sums):
    wide = 2 * z.feats
    return both_halves(sums[:, :wide]) - both_halves(s.pair[here, :].astype(F32)) * sums[:, wide : wide + 1]


def column_terms(total):
    pair = paired(total)
    return pair.T, pair


def column_backprop(z, s, w, pack_ref):
    def first(here, terms):
        t_stack, pair = terms
        g = mm(beside([pair, pair]), w.back[...])
        both = mm(beside([t_stack, t_stack]), jnp.concatenate([s.h1[here, :], s.h2[here, :]], 0))
        pack_ref[: z.feats] += both[: z.feats] + both[z.feats :]
        return g

    def second(here, g):
        g = g * s.slope[here, :]
        x_stack = stack(split(s.x[:, here]))
        g1 = g.astype(BF)
        g2 = (g - g1.astype(F32)).astype(BF)
        both = mm(beside([x_stack, x_stack]), jnp.concatenate([g1, g2], 0))
        pack_ref[z.feats :] += both[: z.ins] + both[z.ins :]

    return first, second


def window_backprop(z, s, w, pack_ref):
    def first(lanes, t_stack):
        g = mm(w.back[...], jnp.concatenate([t_stack, t_stack], 0))
        both = mm_nt(beside([t_stack, t_stack]), beside([s.h1[:, lanes], s.h2[:, lanes]]))
        pack_ref[: z.feats] += both[: z.feats] + both[z.feats :]
        return g

    def second(lanes, g):
        h = s.h1[:, lanes].astype(F32) + s.h2[:, lanes].astype(F32)
        g = g * (1.0 - h * h)
        x_stack = stack(split(s.x[:, lanes]))
        g1 = g.astype(BF)
        g2 = (g - g1.astype(F32)).astype(BF)
        both = mm_nt(beside([x_stack, x_stack]), beside([g1, g2]))
        pack_ref[z.feats :] += both[: z.ins] + both[z.ins :]

    return first, second


def column_steps(z, step):
    return [pl.ds(k * step, step) for k in range(z.cols // step)]


def window_steps(z):
    return [pl.ds(k * z.win_step, z.win_step) for k in range(z.wide // z.win_step)]


def column_features(z, blocks_ref, col, win, w, w_win=None):
    column_blocks(z, blocks_ref, col)
    into, middle, out = column_network(z, col, w)
    first, second = tile(z, win, col, z.early_step)
    lanes = column_steps(z, z.early_step)
    rows = window_steps(z) if w_win else []
    stages = window_network(z, win, w_win) if w_win else ()

    def third(here, raw):
        out(here, raw)
        exact = both_halves(col.pair[here, :].astype(F32))
        norm = 0.25 * jnp.sum(exact * exact, 1, keepdims=True)
        col.norm[here, :] = jnp.broadcast_to(norm, (z.early_step, z.own))
        return first(here)

    def fourth(here, dots):
        col.sums[here, :] = second(here, dots)

    def stage(depth):
        def do(k, value):
            if k >= len(rows):
                here = lanes[k - len(rows)]
                return into(here) if depth == 0 else (middle, third, fourth)[depth - 1](here, value)
            if depth < 3:
                return stages[0](rows[k]) if depth == 0 else stages[depth](rows[k], value)

        return do

    flow(len(rows) + len(lanes), *[stage(depth) for depth in range(4)])


def near_kernel(z, windows_ref, columns_ref, *refs):
    n = len(z.windows())
    w_col, w_win, refs = Refs(WEIGHTS, refs[:3]), Refs(WEIGHTS, refs[3:6]), refs[6:]
    win, col = Refs(z.windows(), refs[:n]), Refs(z.columns(), refs[n:])
    window_blocks(z, windows_ref, win)
    column_features(z, columns_ref, col, win, w_col, w_win)


def far_kernel(z, columns_ref, *refs):
    n, c = len(z.windows()), len(z.columns())
    w_col, refs = Refs(WEIGHTS, refs[:3]), refs[3:]
    win, col = Refs(z.windows(), refs[:n]), Refs(z.columns(), refs[n : n + c])
    sums_ref = refs[n + c]
    sums_ref[...] = win.sums[...]
    win.sums = sums_ref
    column_features(z, columns_ref, col, win, w_col)


def late_kernel(z, windows_ref, *refs):
    n, c = len(z.windows()), len(z.columns())
    w_col, w_win, refs = Refs(WEIGHTS, refs[:3]), Refs(WEIGHTS, refs[3:6]), refs[6:]
    near = Refs(z.windows(), refs[:n])
    cols = [Refs(z.columns(), refs[n : n + c]), Refs(z.columns(), refs[n + c : n + 2 * c])]
    near.sums, col_grad_ref, pack_ref = refs[n + 2 * c : n + 2 * c + 3]
    win = Refs(z.windows(), refs[n + 2 * c + 3 :])
    pack_ref[...] = jnp.zeros(pack_ref.shape, F32)
    rows = window_steps(z)

    def of_window(s, here):
        first, second = window_backprop(z, s, w_win, pack_ref)
        return lambda: first(here, window_terms(z, s, here)), lambda g: second(here, g)

    def of_columns(s, here, total):
        first, second = column_backprop(z, s, w_col, pack_ref)
        return lambda: first(here, column_terms(total)), lambda g: second(here, g)

    window_blocks(z, windows_ref, win)
    into, middle, out = window_network(z, win, w_win)
    for here in rows:
        first, second = of_window(near, here)
        value = into(here)
        other = first()
        value = middle(here, value)
        second(other)
        out(here, value)
    work = [(col, lanes) for col in cols for lanes in column_steps(z, z.col_step)]
    totals = []

    def total(k, dots):
        col, lanes = work[k]
        sums = col.sums[lanes, :] + tile(z, win, col, z.col_step)[1](lanes, dots)
        totals.append(column_total(z, col, lanes, sums))

    flow(len(work), lambda k, _: tile(z, win, work[k][0], z.col_step)[0](work[k][1]), total)
    col_grad_ref[...] = totals[0][: z.own].T[: z.feats]
    stages = [of_columns(*item, t) for item, t in zip(work, totals)] + [of_window(win, here) for here in rows]
    flow(len(stages), lambda k, _: stages[k][0](), lambda k, g: stages[k][1](g))


def emit_kernel(own_ref, col_grad_ref):
    col_grad_ref[...] = own_ref[...]


def finish_kernel(z, mine_ref, theirs_ref, grad_in_ref, grad_bias_ref, grad_out_ref):
    both = mine_ref[...] + theirs_ref[...]
    grad_out_ref[...] = both[: z.feats]
    grad_in_ref[...] = both[z.feats : z.feats + z.depth]
    grad_bias_ref[...] = both[z.feats + z.depth : z.feats + z.depth + 1]


def whole(count):
    return [pl.BlockSpec(memory_space=VMEM)] * count


def shapes(spec):
    return [jax.ShapeDtypeStruct(*v) for v in spec.values()]


def call(kernel, name, outs, operands, scratch=(), limit=4, cost=1, place=VMEM):
    return pl.pallas_call(
        kernel,
        out_shape=tuple(outs),
        in_specs=[pl.BlockSpec(memory_space=place)] * len(operands),
        out_specs=tuple(whole(len(outs))),
        scratch_shapes=list(scratch),
        compiler_params=pltpu.CompilerParams(vmem_limit_bytes=limit << 20),
        cost_estimate=pl.CostEstimate(flops=cost * 10**8, bytes_accessed=10**6, transcendentals=0),
        name=name,
    )(*operands)


def body(n_row, n_col, protocols, w_in, b_in, w_out, solved, probes, window_blocks):
    depth, own = protocols.shape
    z = Sizes(depth, solved.shape[0], w_out.shape[0], w_out.shape[1], own, n_row)
    bits = bits_of(n_col)
    joined = bits[-1]
    shared = [bit for bit in bits if bit != joined]
    limit = 12 if n_row <= 4 else 48
    f32 = functools.partial(jax.ShapeDtypeStruct, dtype=F32)

    theirs = swap(protocols, "col", n_col, 1), swap(solved, "col", n_col, 1)
    blk = f32((z.part, own))
    window, columns, apart = call(
        functools.partial(prepare_kernel, z),
        "prepare",
        (blk, blk, jax.ShapeDtypeStruct((8, own), jnp.int32)),
        [pltpu.with_memory_space_constraint(v, pltpu.HBM) for v in (window_blocks, protocols, solved, probes)],
        [pltpu.SMEM(window_blocks.shape, jnp.int32), pltpu.SemaphoreType.DMA((4,))],
        place=pltpu.HBM,
    )
    (window,) = call(functools.partial(pick_kernel, z), "pick", (blk,), (window, apart, *theirs))

    def nearer(bit, mine, theirs):
        return jnp.where((apart[:1] & bit) == 0, mine, theirs)

    window, w_in, b_in, w_out = lax.optimization_barrier((window, w_in, b_in, w_out))
    forms = ((6 * z.ins, z.hid), (2 * z.hid, 2 * z.feats), (4 * z.feats, z.hid))
    forms += ((z.hid, 6 * z.ins), (2 * z.feats, z.hid), (z.hid, 4 * z.feats))
    weights = call(
        functools.partial(weights_kernel, z),
        "weights",
        [jax.ShapeDtypeStruct(form, BF) for form in forms],
        (w_in[None], b_in.reshape(1, -1), w_out.T),
    )
    got = swap(jnp.concatenate([window, columns]), "col", n_col, joined)
    window = nearer(joined, window, got[: z.part])
    columns = jnp.concatenate([columns, got[z.part :]])
    window, *weights = lax.optimization_barrier((window, *weights))
    for bit in reversed(bits_of(n_row)[1:]):
        columns = jnp.concatenate([columns, swap(columns, "row", n_row, bit)])
    far_columns = swap(columns, "row", n_row, 1)
    for bit in shared[1:]:
        window = nearer(bit, window, swap(window, "col", n_col, bit))
    for bit in reversed(bits_of(n_row)[1:]):
        window = jnp.concatenate([window, swap(window, "row", n_row, bit)])
    far_window = swap(window, "row", n_row, 1)

    near = call(
        functools.partial(near_kernel, z),
        "near",
        (*shapes(z.windows()), *shapes(z.columns())),
        (window, columns, *weights),
        limit=limit,
        cost=10,
    )
    windows, near = near[: len(z.windows())], near[len(z.windows()) :]
    *far, sums = call(
        functools.partial(far_kernel, z),
        "far",
        (*shapes(z.columns()), jax.ShapeDtypeStruct(*z.windows()["sums"])),
        (far_columns, *weights[:3], *windows),
        limit=limit,
        cost=10,
    )
    col_grad, pack = call(
        functools.partial(late_kernel, z),
        "late",
        (f32((z.feats, own)), f32((z.feats + z.ins, z.hid))),
        (far_window, *weights, *windows, *near, *far, sums),
        [VMEM(*v) for v in z.windows().values()],
        limit=limit,
        cost=20,
    )
    for bit in reversed(shared[1:]):
        pack = pack + swap(pack, "col", n_col, bit)
    (col_grad,) = call(emit_kernel, "emit", (f32((z.feats, own)),), (col_grad,))
    grad_in, grad_bias, grad_out = call(
        functools.partial(finish_kernel, z),
        "finish",
        (f32((depth, z.hid)), f32((1, z.hid)), f32((z.feats, z.hid))),
        (pack, swap(pack, "col", n_col, shared[0])),
    )
    return (col_grad, grad_in, grad_bias.reshape(-1), grad_out.T)


def solution(mesh):
    n_row, n_col = mesh.shape["row"], mesh.shape["col"]
    cut = P(None, ("row", "col"))

    def per_device(*args):
        return body(n_row, n_col, *args)

    return jax.shard_map(
        per_device,
        mesh=mesh,
        in_specs=(cut, P(), P(), P(), cut, cut, P()),
        out_specs=(cut, P(), P(), P()),
        check_vma=False,
    )
```
